256 devices in a mesh: tensor: 8 (over y, core), context: 32 (over x, z).
Axes of the slice: x: 4, y: 4, z: 8, core: 2. Of those that a mesh axis runs over, the one named last changes fastest.
Arguments:
- normed_input: bfloat16 [128, 128, 3072], P('context', 'tensor'), may hold values from -6 to 6
- w_qkv: bfloat16 [3072, 3, 2048], P(None, None, 'tensor'), may hold values from -0.109375 to 0.109375
- queries: bfloat16 [16384, 2048], P('context', 'tensor'), may hold values from -9.4 to 9.4
- saved_keys: bfloat16 [16384, 2048], P('context', 'tensor'), may hold values from -9.4 to 9.4
- values: bfloat16 [16384, 2048], P('context', 'tensor'), may hold values from -6 to 6
- attn_out: bfloat16 [16384, 2048], P('context', 'tensor'), may hold values from -6 to 6
- grad_out: bfloat16 [16384, 2048], P('context', 'tensor'), may hold values from -6 to 6
- window_tiles: int32 [128, 24], replicated, may hold values from -1 to 127, as said below
Outputs:
- grad_input: bfloat16 [128, 128, 3072], P('context', 'tensor')
- grad_w: float32 [3072, 3, 2048], P('context', None, 'tensor')
The draws below stay inside these ranges and needn't reach their ends.
Inputs may be any that keep to these rules, and one draw needn't show every extreme that they name: `window_tiles`: row t lists in increasing order the key tiles that query tile t attends to, then -1 in its remaining entries; t itself is always listed, and every listed tile k has |k // 8 - t // 8| <= 1.
All inputs are finite; a program needn't handle non-finite values.
Results may differ from the reference program's by a relative error of at most 0.024.
Values may be sent and summed in bfloat16 or wider, within the bound.
A program may use at most 128 MiB of HBM per device.

```python
import math
import jax
import jax.numpy as jnp
from jax import lax

D = 3072
HEADS = 16
HD = 128
TILE = 128
TILES_FRAME = 8
TILES = 128
TOKENS = 16384
NB = 24
N_CONTEXT = 32


def query_key_pair(key):
    base = jax.random.fold_in(key, 4051)
    key_q, key_k = jax.random.split(base, 2)
    query_vals = jnp.clip(jax.random.normal(key_q, (TOKENS, HEADS * HD), jnp.float32), -4.0, 4.0)
    key_vals = jnp.clip(jax.random.normal(key_k, (TOKENS, HEADS * HD), jnp.float32), -4.0, 4.0)
    return (query_vals, key_vals)


def draw_queries(key, part):
    return query_key_pair(key)[0].astype(jnp.bfloat16)


def draw_saved_keys(key, part):
    return query_key_pair(key)[1].astype(jnp.bfloat16)


def draw_window_tiles(key, part):
    tile_ids = jnp.arange(TILES, dtype=jnp.int32)
    frame = tile_ids // TILES_FRAME
    band = tile_ids % TILES_FRAME // 2
    frame_reach = jax.random.randint(jax.random.fold_in(key, 7), (TILES,), 0, 2, dtype=jnp.int32)
    band_reach = jax.random.randint(jax.random.fold_in(key, 8), (TILES,), 1, 3, dtype=jnp.int32)
    allowed = (jnp.abs(frame[:, None] - frame[None, :]) <= frame_reach[:, None]) & (jnp.abs(band[:, None] - band[None, :]) <= band_reach[:, None])
    ranked = jnp.where(allowed, tile_ids[None, :], TILES + tile_ids[None, :])
    ordered = jnp.sort(ranked, axis=1)[:, :NB]
    return jnp.where(ordered < TILES, ordered, -1).astype(jnp.int32)


def spiked(array, key, source, target, blocks, factor):
    owner, partner = [(jnp.arange(array.shape[dim]) // (array.shape[dim] // blocks)).reshape([-1 if axis == dim else 1 for axis in range(array.ndim)]) for dim in (source, target)]
    chosen = jax.random.permutation(key, blocks)[partner]
    strong = (owner == chosen) | (owner == (partner + blocks // 2) % blocks)
    return jnp.where(strong, factor * array, array)


def steps_of(key, shape, cuts, least, high):
    factor_of = 1.0
    for dim, parts in cuts:
        steps = jax.random.uniform(jax.random.fold_in(jax.random.fold_in(key, 6), dim), (parts,), jnp.float32, least / len(cuts), high / len(cuts))
        factor_of = factor_of * jnp.repeat(jnp.exp(steps), shape[dim] // parts).reshape((-1,) + (1,) * (len(shape) - 1 - dim))
    return factor_of


def centred(rng, dims, width, bound, cuts=(), kind=jnp.bfloat16):
    array = jax.random.normal(rng, dims, jnp.float32) * width
    if len(cuts) > 0:
        array = steps_of(rng, dims, cuts, -0.22, 0.18) * array
    return jnp.clip(array, min=-bound, max=bound).astype(kind)


def noise_with(stream_key, extent, spread, reach, shards, heavy, kind=jnp.bfloat16):
    result = spread * jax.random.normal(stream_key, extent, jnp.float32)
    if shards:
        result = result * steps_of(stream_key, extent, shards, -0.22, 0.18)
    return jnp.clip(spiked(result, jax.random.fold_in(stream_key, 3), *heavy), -reach, reach).astype(kind)


def setup_inputs(seed: int = 0) -> dict:
    seeds = jax.random.split(jax.random.key(seed), 9)
    normed_input = noise_with(seeds[0], (TILES, TILE, D), 1.0, 6.0, ((0, 32), (1, 8)), (0, 2, 32, 2.75))
    w_qkv = centred(seeds[1], (D, 3, HEADS * HD), D ** -0.5, 0.109375, ((2, 8),))
    queries = draw_queries(jax.random.fold_in(seeds[8], 71), 0)
    saved_keys = draw_saved_keys(jax.random.fold_in(seeds[8], 71), 0)
    values = centred(seeds[4], (TOKENS, HEADS * HD), 1.0, 6.0, ((0, 32), (1, 8)))
    attn_out = centred(seeds[5], (TOKENS, HEADS * HD), 1.0, 6.0, ((0, 32), (1, 8)))
    grad_out = centred(seeds[6], (TOKENS, HEADS * HD), 1.0, 6.0, ((0, 32), (1, 8)))
    window_tiles = draw_window_tiles(jax.random.fold_in(seeds[8], 71), 0)
    return dict(normed_input=normed_input, w_qkv=w_qkv, queries=queries, saved_keys=saved_keys, values=values, attn_out=attn_out, grad_out=grad_out, window_tiles=window_tiles)


def reference(normed_input, w_qkv, queries, saved_keys, values, attn_out, grad_out, window_tiles):
    scale = 1.0 / math.sqrt(HD)
    tile_ids = jnp.arange(TILES, dtype=jnp.int32)
    tile_allowed = jnp.any(window_tiles[:, :, None] == tile_ids[None, None, :], axis=1)
    allowed = jnp.repeat(jnp.repeat(tile_allowed, TILE, axis=0), TILE, axis=1)

    def split_heads(arr):
        return arr.reshape(TOKENS, HEADS, HD).transpose(1, 0, 2)

    def one_head(group):
        query_h, key_h, value_h, output_h, cot_h = group
        scores = jnp.dot(query_h, key_h.T, preferred_element_type=jnp.float32) * scale
        masked = jnp.where(allowed, scores, -1e+30)
        row_max = lax.optimization_barrier(jnp.max(masked, axis=1, keepdims=True))
        row_sum = lax.optimization_barrier(jnp.sum(jnp.exp(masked - row_max), axis=1, keepdims=True))
        lse = row_max + jnp.log(row_sum)
        probs = jnp.where(allowed, jnp.exp(scores - lse), 0.0)
        probs_b = probs.astype(jnp.bfloat16)
        grad_v = jnp.dot(probs_b.T, cot_h, preferred_element_type=jnp.float32)
        dprobs = jnp.dot(cot_h, value_h.T, preferred_element_type=jnp.float32)
        delta = lax.optimization_barrier(jnp.sum(cot_h.astype(jnp.float32) * output_h.astype(jnp.float32), axis=1, keepdims=True))
        dscores = (probs * (dprobs - delta)).astype(jnp.bfloat16)
        grad_q = jnp.dot(dscores, key_h, preferred_element_type=jnp.float32) * scale
        grad_k = jnp.dot(dscores.T, query_h, preferred_element_type=jnp.float32) * scale
        return (grad_q.astype(jnp.bfloat16), grad_k.astype(jnp.bfloat16), grad_v.astype(jnp.bfloat16))
    grad_q, grad_k, grad_v = lax.map(one_head, (split_heads(queries), split_heads(saved_keys), split_heads(values), split_heads(attn_out), split_heads(grad_out)))

    def join_heads(arr):
        return arr.transpose(1, 0, 2).reshape(TOKENS, HEADS * HD)
    grad_qkv = jnp.stack([join_heads(grad_q), join_heads(grad_k), join_heads(grad_v)], axis=1)
    flat_grad = grad_qkv.reshape(TOKENS, 3 * HEADS * HD)
    flat_w = w_qkv.reshape(D, 3 * HEADS * HD)
    grad_input = jnp.dot(flat_grad, flat_w.T, preferred_element_type=jnp.float32).astype(jnp.bfloat16)
    grad_input = grad_input.reshape(TILES, TILE, D)
    block_rows = TOKENS // N_CONTEXT
    input_blocks = normed_input.reshape(N_CONTEXT, block_rows, D)
    grad_blocks = flat_grad.reshape(N_CONTEXT, block_rows, 3 * HEADS * HD)

    def add_block(total, pair):
        part = jnp.dot(pair[0].T, pair[1], preferred_element_type=jnp.float32).astype(jnp.bfloat16)
        part = lax.optimization_barrier(part)
        return (total + part.astype(jnp.float32), None)
    grad_w, unused = lax.scan(add_block, jnp.zeros((D, 3 * HEADS * HD), jnp.float32), (input_blocks, grad_blocks))
    return (grad_input, grad_w.reshape(D, 3, HEADS * HD))
```

```python
import functools
import math

import jax
import jax.numpy as jnp
from jax import lax
from jax.experimental import pallas as pl
from jax.experimental.pallas import tpu as pltpu
from jax.sharding import PartitionSpec as P

D = 3072
HD = 128
TILE = 128
NX, NZ, NY, NK = 4, 8, 4, 2
NT, NC = NY * NK, NX * NZ
HEADS = 2
WIDTH = HEADS * HD
TILES = 4
ROWS = TILES * TILE
QUERIES = 2 * ROWS
SLOTS = 3
KEYS = SLOTS * ROWS
SHARE = TILE // NT
DX = D // NX
DZ = DX // NZ
CHUNK = 256
SCALE = 1.0 / math.sqrt(HD)
LOG2E = 1.4426950408889634
MASKED = -1e30
MESH = pl.DeviceIdType.MESH
NN = (((1,), (0,)), ((), ()))
NTR = (((1,), (1,)), ((), ()))
F32 = jnp.float32
BF16 = jnp.bfloat16


def dot(a, b, dims):
    return lax.dot_general(a, b, dims, preferred_element_type=F32)


def kernel(
    q_ref, k_ref, v_ref, o_ref, do_ref, x_ref, w_ref, wt_ref,
    gi_ref, gw_ref,
    qb, dob, kb, vb, e_ref, dp_ref, bias, mx, lx, rx, delta, st_send, st_recv,
    dkv_send, dkv_recv, dkv_own, dqt, dq_send, dq_recv, g_ref,
    xa, xg, xt, wv, gwp, gwr, gip, gis, gia, gir,
    send, recv, local,
):
    t, c = lax.axis_index("tensor"), lax.axis_index("context")
    x, z = c // NZ, c % NZ
    y, k = t // NK, t % NK
    side = 2 * (c % 2) - 1
    partner = c - side
    near = (c + side + NC) % NC
    far = (c + 2 * side + NC) % NC
    far_user = (c - 2 * side + NC) % NC

    def x_peer(r):
        return (t, ((x + r) % NX) * NZ + z)

    def z_peer(r):
        return (t, x * NZ + (z + r) % NZ)

    def y_peer(r):
        return (((y + r) % NY) * NK + k, c)

    sibling = (y * NK + 1 - k, c)

    barrier = pltpu.get_barrier_semaphore()
    peers = [(t, near), (t, far), (t, far_user), sibling]
    peers += [x_peer(r) for r in range(1, NX)]
    peers += [z_peer(r) for r in range(1, NZ)]
    peers += [y_peer(r) for r in range(1, NY)]
    for peer in peers:
        pl.semaphore_signal(barrier, inc=1, device_id=peer, device_id_type=MESH)
    pl.semaphore_wait(barrier, len(peers))

    started = []

    def push(src, dst, device):
        number = len(started)
        copy = pltpu.make_async_remote_copy(
            src_ref=src,
            dst_ref=dst,
            send_sem=send.at[number],
            recv_sem=recv.at[number],
            device_id=device,
            device_id_type=MESH,
        )
        copy.start()
        started.append(copy)
        return copy

    to_partner = [
        push(q_ref, qb.at[pl.ds(ROWS, ROWS)], (t, partner)),
        push(do_ref, dob.at[pl.ds(ROWS, ROWS)], (t, partner)),
    ]
    to_near = [push(k_ref, kb.at[1], (t, near)), push(v_ref, vb.at[1], (t, near))]
    to_far = [push(k_ref, kb.at[2], (t, far_user)), push(v_ref, vb.at[2], (t, far_user))]
    x_first = [
        push(x_ref.at[:, :, pl.ds(((x + r) % NX) * DX, DX)], xa.at[x], x_peer(r))
        for r in range(1, NX)
    ]
    x_own = pltpu.make_async_copy(x_ref.at[:, :, pl.ds(x * DX, DX)], xa.at[x], local.at[0])
    x_own.start()
    w_copy = pltpu.make_async_copy(w_ref, wv, local.at[1])
    w_copy.start()

    qb[pl.ds(0, ROWS), :] = q_ref[...]
    dob[pl.ds(0, ROWS), :] = do_ref[...]
    kb[0] = k_ref[...]
    vb[0] = v_ref[...]

    window = wt_ref[...]
    first_tiles = [c * TILES, near * TILES, far * TILES]
    hits = [
        jnp.max(jnp.where(window == first + i, 1.0, 0.0), axis=0, keepdims=True)
        for first in first_tiles
        for i in range(TILES)
    ]
    hits = jnp.concatenate(hits + [jnp.zeros((4, NC * TILES), F32)], axis=0)
    column = lax.broadcasted_iota(jnp.int32, (NC * TILES, QUERIES), 1) // TILE
    entry = lax.broadcasted_iota(jnp.int32, (NC * TILES, QUERIES), 0)
    wanted = jnp.where(column < TILES, c * TILES + column, partner * TILES + column - TILES)
    pick = jnp.where(entry == wanted, 1.0, 0.0)
    bias[...] = (1.0 - dot(hits.astype(BF16), pick.astype(BF16), NN)) * MASKED

    st_send[...] = jnp.zeros_like(st_send)
    for h in range(HEADS):
        cols = pl.ds(h * HD, HD)
        product = do_ref[:, cols].astype(F32) * o_ref[:, cols].astype(F32)
        row = jnp.sum(product.T, axis=0, keepdims=True)
        delta[h, :, pl.ds(0, ROWS)] = row
        st_send[4 + h, :, pl.ds(0, ROWS)] = row

    def score_block(slot, first, count):
        def step(i, carry):
            h = i // count
            cols = pl.ds(pl.multiple_of((first + i % count) * CHUNK, CHUNK), CHUNK)
            head = pl.ds(pl.multiple_of(h * HD, HD), HD)
            s = dot(kb[slot, :, head], qb[cols, head], NTR) * (SCALE * LOG2E)
            parts = [
                s[i * TILE : (i + 1) * TILE] + bias[pl.ds(slot * TILES + i, 1), cols]
                for i in range(TILES)
            ]
            top = functools.reduce(jnp.maximum, parts)
            top = jnp.max(top, axis=0, keepdims=True)
            total = None
            for i, part in enumerate(parts):
                e = jnp.exp2(part - top)
                e_ref[h, pl.ds(slot * ROWS + i * TILE, TILE), cols] = e
                total = e if total is None else total + e
            mx[h * SLOTS + slot, :, cols] = top
            lx[h * SLOTS + slot, :, cols] = jnp.sum(total, axis=0, keepdims=True)
            return carry

        lax.fori_loop(0, HEADS * count, step, 0)

    def dprob_block(slot, first, count):
        def step(i, carry):
            h = i // count
            cols = pl.ds(pl.multiple_of((first + i % count) * CHUNK, CHUNK), CHUNK)
            head = pl.ds(pl.multiple_of(h * HD, HD), HD)
            dp_ref[h, pl.ds(slot * ROWS, ROWS), cols] = dot(vb[slot, :, head], dob[cols, head], NTR)
            return carry

        lax.fori_loop(0, HEADS * count, step, 0)

    half = ROWS // CHUNK
    score_block(0, 0, half)
    dprob_block(0, 0, half)

    x_own.wait()
    for copy in x_first:
        copy.wait_recv()
    x_second = [push(xa, xg.at[:, :, t], y_peer(r)) for r in range(1, NY)]
    x_side = [push(xa, xg.at[:, :, t], sibling)]
    x_place = pltpu.make_async_copy(xa, xg.at[:, :, t], local.at[2])
    x_place.start()

    for copy in to_partner:
        copy.wait_recv()
    score_block(0, half, half)
    dprob_block(0, half, half)
    for copy in to_near:
        copy.wait_recv()
    score_block(1, 0, 2 * half)
    dprob_block(1, 0, 2 * half)

    for r, copy in zip(range(1, NY), x_second):
        copy.wait_recv()
        origin = ((y - r + NY) % NY) * NK + k
        x_side.append(push(xg.at[:, :, origin], xg.at[:, :, origin], sibling))

    for copy in to_far:
        copy.wait_recv()
    score_block(2, 0, 2 * half)

    for h in range(HEADS):
        tops = [mx[h * SLOTS + j] for j in range(SLOTS)]
        top = functools.reduce(jnp.maximum, tops)
        total = sum(lx[h * SLOTS + j] * jnp.exp2(tops[j] - top) for j in range(SLOTS))
        st_send[h] = top
        st_send[2 + h] = total
    stats = push(st_send, st_recv, (t, partner))
    dprob_block(2, 0, 2 * half)
    stats.wait_recv()
    for h in range(HEADS):
        delta[h, :, pl.ds(ROWS, ROWS)] = st_recv[4 + h, :, pl.ds(0, ROWS)]
        for u in range(2):
            mine, theirs = pl.ds(u * ROWS, ROWS), pl.ds((1 - u) * ROWS, ROWS)
            top_a, top_b = st_send[h, :, mine], st_recv[h, :, theirs]
            top = jnp.maximum(top_a, top_b)
            total = st_send[2 + h, :, mine] * jnp.exp2(top_a - top)
            total = total + st_recv[2 + h, :, theirs] * jnp.exp2(top_b - top)
            lse = top + jnp.log2(total)
            for j in range(SLOTS):
                rx[h * SLOTS + j, :, mine] = jnp.exp2(mx[h * SLOTS + j, :, mine] - lse)

    dqt[...] = jnp.zeros_like(dqt)

    def grad_block(slot):
        def step(i, carry):
            h = i // 2
            part = pl.multiple_of((i % 2) * CHUNK, CHUNK)
            head = pl.ds(pl.multiple_of(h * HD, HD), HD)
            here = pl.ds(part, CHUNK)
            rows = pl.ds(slot * ROWS + part, CHUNK)
            keys_t = kb[slot, here, head].T
            grad_k = grad_v = None
            for u in range(2):
                cols = pl.ds(u * ROWS, ROWS)
                p = e_ref[h, rows, cols] * rx[h * SLOTS + slot, :, cols]
                ds = (p * (dp_ref[h, rows, cols] - delta[h, :, cols])).astype(BF16)
                dv = dot(p.astype(BF16), dob[cols, head], NN)
                dk = dot(ds, qb[cols, head], NN)
                grad_v = dv if grad_v is None else grad_v + dv
                grad_k = dk if grad_k is None else grad_k + dk
                dqt[h, :, cols] += dot(keys_t, ds, NN)
            if slot == 0:
                dkv_own[0, here, head] = grad_k * SCALE
                dkv_own[1, here, head] = grad_v
            else:
                dkv_send[2 * slot - 2, here, head] = (grad_k * SCALE).astype(BF16)
                dkv_send[2 * slot - 1, here, head] = grad_v.astype(BF16)
            return carry

        lax.fori_loop(0, HEADS * 2, step, 0)

    grad_block(2)
    returns = [push(dkv_send.at[2 + a], dkv_recv.at[2 + a], (t, far)) for a in range(2)]
    grad_block(1)
    returns += [push(dkv_send.at[a], dkv_recv.at[a], (t, near)) for a in range(2)]
    grad_block(0)
    for h in range(HEADS):
        dq_send[:, pl.ds(h * HD, HD)] = (dqt[h, :, pl.ds(ROWS, ROWS)] * SCALE).T.astype(BF16)
    dq_swap = push(dq_send, dq_recv, (t, partner))

    x_place.wait()
    for copy in x_side:
        copy.wait_recv()

    def turn(i, carry):
        for u in range(2):
            block = xg[i // 2, (i % 2) * 2 + u].reshape(TILE, DX)
            xt[:, pl.ds(pl.multiple_of(i * 2 * TILE, 2 * TILE) + u * TILE, TILE)] = block.T
        return carry

    lax.fori_loop(0, NX * TILES // 2, turn, 0)

    def gather(a):
        return [push(g_ref.at[a, x], g_ref.at[a, x], x_peer(r)) for r in range(1, NX)]

    def weight_share(a):
        def step(i, carry):
            rows = pl.ds(pl.multiple_of(i * 2 * DZ, 2 * DZ), 2 * DZ)
            part = dot(xt[rows, :], g_ref[a].reshape(NX * ROWS, WIDTH), NN)
            gwp[a, pl.ds(2 * i, 2)] = part.reshape(2, DZ, WIDTH).astype(BF16)
            return carry

        lax.fori_loop(0, NZ // 2, step, 0)
        return [push(gwp.at[a, (z + r) % NZ], gwr.at[a, z], z_peer(r)) for r in range(1, NZ)]

    dq_swap.wait_recv()
    for h in range(HEADS):
        cols = pl.ds(h * HD, HD)
        own = (dqt[h, :, pl.ds(0, ROWS)] * SCALE).T + dq_recv[:, cols].astype(F32)
        g_ref[0, x, :, :, :, :, cols] = own.astype(BF16).reshape(TILES, NY, NK, SHARE, HD)
    gathers = [gather(0)]
    for copy in gathers[0]:
        copy.wait_recv()
    shares = weight_share(0)

    for copy in returns:
        copy.wait_recv()
    for a in range(2):
        total = dkv_own[a] + dkv_recv[a].astype(F32) + dkv_recv[2 + a].astype(F32)
        g_ref[1 + a, x] = total.astype(BF16).reshape(TILES, NY, NK, SHARE, WIDTH)
        gathers.append(gather(1 + a))

    w_copy.wait()

    def input_share(core):
        def step(i, carry):
            cols = pl.ds(pl.multiple_of(i * 512, 512), 512)
            part = sum(
                dot(
                    g_ref[a, x, :, :, core].reshape(TILES * NY * SHARE, WIDTH),
                    wv[a, cols, :],
                    NTR,
                )
                for a in range(3)
            )
            gip[core, :, :, :, cols] = part.astype(BF16).reshape(TILES, NY, SHARE, 512)
            return carry

        lax.fori_loop(0, D // 512, step, 0)

    input_share(1 - k)
    cross = push(gip.at[1 - k], gis, sibling)
    input_share(k)

    for a in (1, 2):
        for copy in gathers[a]:
            copy.wait_recv()
        shares += weight_share(a)

    cross.wait_recv()

    def add_cores(i, carry):
        gia[i] = (gip[k, i].astype(F32) + gis[i].astype(F32)).astype(BF16)
        return carry

    lax.fori_loop(0, TILES, add_cores, 0)
    spread = [push(gia.at[:, (y + r) % NY], gir.at[r - 1], y_peer(r)) for r in range(1, NY)]

    for copy in shares:
        copy.wait_recv()
    for a in range(3):
        total = gwp[a, z].astype(F32)
        for r in range(1, NZ):
            total = total + gwr[a, (z + r) % NZ].astype(F32)
        gw_ref[a] = total

    for copy in spread:
        copy.wait_recv()

    def add_chips(i, carry):
        total = gia[i, y].astype(F32)
        for r in range(NY - 1):
            total = total + gir[r, i].astype(F32)
        gi_ref[i] = total.astype(BF16)
        return carry

    lax.fori_loop(0, TILES, add_chips, 0)

    for copy in started:
        copy.wait_send()


N_COPIES = 6 + 3 + 3 + 4 + 1 + 4 + 1 + 3 * (NX - 1) + 3 * (NZ - 1) + 1 + 3


def body(normed_input, w_qkv, queries, saved_keys, values, attn_out, grad_out, window_tiles):
    vmem = pl.BlockSpec(memory_space=pltpu.VMEM)
    anywhere = pl.BlockSpec(memory_space=pl.ANY)
    block = (ROWS, WIDTH)
    grads = (3, NX, TILES, NY, NK, SHARE, WIDTH)
    scratch = [
        ((QUERIES, WIDTH), BF16),
        ((QUERIES, WIDTH), BF16),
        ((SLOTS, *block), BF16),
        ((SLOTS, *block), BF16),
        ((HEADS, KEYS, QUERIES), F32),
        ((HEADS, KEYS, QUERIES), F32),
        ((16, QUERIES), F32),
        ((HEADS * SLOTS, 1, QUERIES), F32),
        ((HEADS * SLOTS, 1, QUERIES), F32),
        ((HEADS * SLOTS, 1, QUERIES), F32),
        ((HEADS, 1, QUERIES), F32),
        ((6, 1, QUERIES), F32),
        ((6, 1, QUERIES), F32),
        ((4, *block), BF16),
        ((4, *block), BF16),
        ((2, *block), F32),
        ((HEADS, HD, QUERIES), F32),
        (block, BF16),
        (block, BF16),
        (grads, BF16),
        ((NX, TILES, SHARE, DX), BF16),
        ((NX, TILES, NT, SHARE, DX), BF16),
        ((DX, NX * ROWS), BF16),
        ((3, D, WIDTH), BF16),
        ((3, NZ, DZ, WIDTH), BF16),
        ((3, NZ, DZ, WIDTH), BF16),
        ((NK, TILES, NY, SHARE, D), BF16),
        ((TILES, NY, SHARE, D), BF16),
        ((TILES, NY, SHARE, D), BF16),
        ((NY - 1, TILES, SHARE, D), BF16),
    ]
    grad_input, grad_w = pl.pallas_call(
        kernel,
        out_shape=[
            jax.ShapeDtypeStruct((TILES, SHARE, D), BF16),
            jax.ShapeDtypeStruct((3, DZ, WIDTH), F32),
        ],
        in_specs=[vmem] * 5 + [anywhere] * 2 + [vmem],
        out_specs=[vmem, vmem],
        scratch_shapes=[pltpu.VMEM(shape, kind) for shape, kind in scratch]
        + [
            pltpu.SemaphoreType.DMA((N_COPIES,)),
            pltpu.SemaphoreType.DMA((N_COPIES,)),
            pltpu.SemaphoreType.DMA((3,)),
        ],
        compiler_params=pltpu.CompilerParams(
            collective_id=0, has_side_effects=True, vmem_limit_bytes=60 * 2**20
        ),
        name="window_grads",
    )(
        queries,
        saved_keys,
        values,
        attn_out,
        grad_out,
        normed_input,
        w_qkv.transpose(1, 0, 2),
        window_tiles.T,
    )
    return grad_input, grad_w.transpose(1, 0, 2)


def solution(mesh):
    placed = (
        P("context", "tensor", None),
        P(None, None, "tensor"),
        P("context", "tensor"),
        P("context", "tensor"),
        P("context", "tensor"),
        P("context", "tensor"),
        P("context", "tensor"),
        P(),
    )
    return jax.shard_map(
        body,
        mesh=mesh,
        in_specs=placed,
        out_specs=(P("context", "tensor", None), P("context", None, "tensor")),
        check_vma=False,
    )
```

```python
import functools
import math

import jax
import jax.numpy as jnp
from jax import lax
from jax.experimental import pallas as pl
from jax.experimental.pallas import tpu as pltpu
from jax.sharding import PartitionSpec as P

D = 3072
HD = 128
TILE = 128
NX, NZ, NY, NK = 4, 8, 4, 2
NT, NC = NY * NK, NX * NZ
HEADS = 2
WIDTH = HEADS * HD
TILES = 4
ROWS = TILES * TILE
QUERIES = 2 * ROWS
SLOTS = 3
KEYS = SLOTS * ROWS
SHARE = TILE // NT
DX = D // NX
DZ = DX // NZ
CHUNK = 256
SCALE = 1.0 / math.sqrt(HD)
LOG2E = 1.4426950408889634
MASKED = -1e30
MESH = pl.DeviceIdType.MESH
NN = (((1,), (0,)), ((), ()))
NTR = (((1,), (1,)), ((), ()))
F32 = jnp.float32
BF16 = jnp.bfloat16


def dot(a, b, dims):
    return lax.dot_general(a, b, dims, preferred_element_type=F32)


def kernel(
    q_ref, k_ref, v_ref, o_ref, do_ref, x_ref, w_ref, wt_ref,
    gi_ref, gw_ref,
    qb, dob, kb, vb, e_ref, bias, mx, lx, rx, delta, st_send, st_recv,
    dkv_send, dkv_recv, dkv_own, dqt, dq_send, dq_recv, g_ref,
    xy, xg, xt, wv, gwp, gwr, gip, gis, gia, gir,
    send, recv, local,
):
    t, c = lax.axis_index("tensor"), lax.axis_index("context")
    x, z = c // NZ, c % NZ
    y, k = t // NK, t % NK
    side = 2 * (c % 2) - 1
    partner = c - side
    near = (c + side + NC) % NC
    far = (c + 2 * side + NC) % NC
    far_user = (c - 2 * side + NC) % NC

    def x_peer(r):
        return (t, ((x + r) % NX) * NZ + z)

    def z_peer(r):
        return (t, x * NZ + (z + r) % NZ)

    def y_peer(r):
        return (((y + r) % NY) * NK + k, c)

    sibling = (y * NK + 1 - k, c)

    barrier = pltpu.get_barrier_semaphore()
    peers = [(t, near), (t, far), (t, far_user), sibling]
    peers += [x_peer(r) for r in range(1, NX)]
    peers += [z_peer(r) for r in range(1, NZ)]
    peers += [y_peer(r) for r in range(1, NY)]
    for peer in peers:
        pl.semaphore_signal(barrier, inc=1, device_id=peer, device_id_type=MESH)
    pl.semaphore_wait(barrier, len(peers))

    started = []

    def push(src, dst, device):
        number = len(started)
        copy = pltpu.make_async_remote_copy(
            src_ref=src,
            dst_ref=dst,
            send_sem=send.at[number],
            recv_sem=recv.at[number],
            device_id=device,
            device_id_type=MESH,
        )
        copy.start()
        started.append(copy)
        return copy

    x_first = [push(x_ref, xy.at[:, y], y_peer(r)) for r in range(1, NY)]
    q_swap = push(q_ref, qb.at[pl.ds(ROWS, ROWS)], (t, partner))
    k_near = push(k_ref, kb.at[1], (t, near))
    k_far = push(k_ref, kb.at[2], (t, far_user))
    do_swap = push(do_ref, dob.at[pl.ds(ROWS, ROWS)], (t, partner))
    v_near = push(v_ref, vb.at[1], (t, near))
    x_own = pltpu.make_async_copy(x_ref, xy.at[:, y], local.at[0])
    x_own.start()
    w_copy = pltpu.make_async_copy(w_ref, wv, local.at[1])
    w_copy.start()

    qb[pl.ds(0, ROWS), :] = q_ref[...]
    dob[pl.ds(0, ROWS), :] = do_ref[...]
    kb[0] = k_ref[...]
    vb[0] = v_ref[...]

    window = wt_ref[...]
    first_tiles = [c * TILES, near * TILES, far * TILES]
    hits = [
        jnp.max(jnp.where(window == first + i, 1.0, 0.0), axis=0, keepdims=True)
        for first in first_tiles
        for i in range(TILES)
    ]
    hits = jnp.concatenate(hits + [jnp.zeros((4, NC * TILES), F32)], axis=0)
    column = lax.broadcasted_iota(jnp.int32, (NC * TILES, QUERIES), 1) // TILE
    entry = lax.broadcasted_iota(jnp.int32, (NC * TILES, QUERIES), 0)
    wanted = jnp.where(column < TILES, c * TILES + column, partner * TILES + column - TILES)
    pick = jnp.where(entry == wanted, 1.0, 0.0)
    bias[...] = (1.0 - dot(hits.astype(BF16), pick.astype(BF16), NN)) * MASKED

    st_send[...] = jnp.zeros_like(st_send)
    for h in range(HEADS):
        cols = pl.ds(h * HD, HD)
        product = do_ref[:, cols].astype(F32) * o_ref[:, cols].astype(F32)
        row = jnp.sum(product.T, axis=0, keepdims=True)
        delta[h, :, pl.ds(0, ROWS)] = row
        st_send[4 + h, :, pl.ds(0, ROWS)] = row

    def score_block(slot, first, count):
        def step(i, carry):
            h = i // count
            cols = pl.ds(pl.multiple_of((first + i % count) * CHUNK, CHUNK), CHUNK)
            head = pl.ds(pl.multiple_of(h * HD, HD), HD)
            s = dot(kb[slot, :, head], qb[cols, head], NTR) * (SCALE * LOG2E)
            parts = [
                s[i * TILE : (i + 1) * TILE] + bias[pl.ds(slot * TILES + i, 1), cols]
                for i in range(TILES)
            ]
            top = functools.reduce(jnp.maximum, parts)
            top = jnp.max(top, axis=0, keepdims=True)
            total = None
            for i, part in enumerate(parts):
                e = jnp.exp2(part - top)
                e_ref[h, pl.ds(slot * ROWS + i * TILE, TILE), cols] = e
                total = e if total is None else total + e
            mx[h * SLOTS + slot, :, cols] = top
            lx[h * SLOTS + slot, :, cols] = jnp.sum(total, axis=0, keepdims=True)
            return carry

        lax.fori_loop(0, HEADS * count, step, 0)

    half = ROWS // CHUNK
    score_block(0, 0, half)
    q_swap.wait_recv()
    score_block(0, half, half)
    k_near.wait_recv()
    score_block(1, 0, 2 * half)
    k_far.wait_recv()
    score_block(2, 0, 2 * half)

    for h in range(HEADS):
        tops = [mx[h * SLOTS + j] for j in range(SLOTS)]
        top = functools.reduce(jnp.maximum, tops)
        total = sum(lx[h * SLOTS + j] * jnp.exp2(tops[j] - top) for j in range(SLOTS))
        st_send[h] = top
        st_send[2 + h] = total
    stats = push(st_send, st_recv, (t, partner))
    v_far = push(v_ref, vb.at[2], (t, far_user))
    dqt[...] = jnp.zeros_like(dqt)
    stats.wait_recv()
    for h in range(HEADS):
        delta[h, :, pl.ds(ROWS, ROWS)] = st_recv[4 + h, :, pl.ds(0, ROWS)]
        for u in range(2):
            mine, theirs = pl.ds(u * ROWS, ROWS), pl.ds((1 - u) * ROWS, ROWS)
            top_a, top_b = st_send[h, :, mine], st_recv[h, :, theirs]
            top = jnp.maximum(top_a, top_b)
            total = st_send[2 + h, :, mine] * jnp.exp2(top_a - top)
            total = total + st_recv[2 + h, :, theirs] * jnp.exp2(top_b - top)
            lse = top + jnp.log2(total)
            for j in range(SLOTS):
                rx[h * SLOTS + j, :, mine] = jnp.exp2(mx[h * SLOTS + j, :, mine] - lse)

    def grad_block(slot):
        def step(i, carry):
            h = i // 2
            part = pl.multiple_of((i % 2) * CHUNK, CHUNK)
            head = pl.ds(pl.multiple_of(h * HD, HD), HD)
            here = pl.ds(part, CHUNK)
            rows = pl.ds(slot * ROWS + part, CHUNK)
            keys_t = kb[slot, here, head].T
            value = vb[slot, here, head]
            grad_k = grad_v = None
            for u in range(2):
                cols = pl.ds(u * ROWS, ROWS)
                p = e_ref[h, rows, cols] * rx[h * SLOTS + slot, :, cols]
                dp = dot(value, dob[cols, head], NTR)
                ds = (p * (dp - delta[h, :, cols])).astype(BF16)
                dv = dot(p.astype(BF16), dob[cols, head], NN)
                dk = dot(ds, qb[cols, head], NN)
                grad_v = dv if grad_v is None else grad_v + dv
                grad_k = dk if grad_k is None else grad_k + dk
                dqt[h, :, cols] += dot(keys_t, ds, NN)
            if slot == 0:
                dkv_own[0, here, head] = grad_k * SCALE
                dkv_own[1, here, head] = grad_v
            else:
                dkv_send[2 * slot - 2, here, head] = (grad_k * SCALE).astype(BF16)
                dkv_send[2 * slot - 1, here, head] = grad_v.astype(BF16)
            return carry

        lax.fori_loop(0, HEADS * 2, step, 0)

    do_swap.wait_recv()
    v_near.wait_recv()
    grad_block(1)
    dv_near = push(dkv_send.at[1], dkv_recv.at[1], (t, near))
    dk_near = push(dkv_send.at[0], dkv_recv.at[0], (t, near))

    x_own.wait()
    for copy in x_first:
        copy.wait_recv()
    x_second = [
        push(
            xy.at[:, :, :, pl.ds(((x + r) % NX) * DX, DX)], xg.at[x, :, :, k], x_peer(r)
        )
        for r in range(1, NX)
    ]
    x_place = pltpu.make_async_copy(
        xy.at[:, :, :, pl.ds(x * DX, DX)], xg.at[x, :, :, k], local.at[2]
    )
    x_place.start()

    v_far.wait_recv()
    grad_block(2)
    dv_far = push(dkv_send.at[3], dkv_recv.at[3], (t, far))
    dk_far = push(dkv_send.at[2], dkv_recv.at[2], (t, far))
    grad_block(0)
    for h in range(HEADS):
        dq_send[:, pl.ds(h * HD, HD)] = (dqt[h, :, pl.ds(ROWS, ROWS)] * SCALE).T.astype(BF16)
    dq_swap = push(dq_send, dq_recv, (t, partner))

    x_place.wait()
    for copy in x_second:
        copy.wait_recv()
    x_side = push(xg.at[:, :, :, k], xg.at[:, :, :, k], sibling)

    def turn(i, carry):
        for u in range(2):
            block = xg[i // 2, (i % 2) * 2 + u].reshape(TILE, DX)
            xt[:, pl.ds(pl.multiple_of(i * 2 * TILE, 2 * TILE) + u * TILE, TILE)] = block.T
        return carry

    def gather(a):
        return [push(g_ref.at[a, x], g_ref.at[a, x], x_peer(r)) for r in (1, NX - 1)]

    def gather_on(a, first):
        copies = []
        for copy, r, part in zip(first, (1, NX - 1), (0, TILES // 2)):
            copy.wait_recv()
            piece = g_ref.at[a, (x - r + NX) % NX, pl.ds(part, TILES // 2)]
            copies.append(push(piece, piece, x_peer(r)))
        return copies

    def weight_share(a):
        def step(i, carry):
            rows = pl.ds(pl.multiple_of(i * 2 * DZ, 2 * DZ), 2 * DZ)
            part = dot(xt[rows, :], g_ref[a].reshape(NX * ROWS, WIDTH), NN)
            gwp[a, pl.ds(2 * i, 2)] = part.reshape(2, DZ, WIDTH).astype(BF16)
            return carry

        lax.fori_loop(0, NZ // 2, step, 0)
        return [push(gwp.at[a, (z + r) % NZ], gwr.at[a, z], z_peer(r)) for r in range(1, NZ)]

    def join(a):
        total = dkv_own[a] + dkv_recv[a].astype(F32) + dkv_recv[2 + a].astype(F32)
        g_ref[1 + a, x] = total.astype(BF16).reshape(TILES, NY, NK, SHARE, WIDTH)

    dq_swap.wait_recv()
    for h in range(HEADS):
        cols = pl.ds(h * HD, HD)
        own = (dqt[h, :, pl.ds(0, ROWS)] * SCALE).T + dq_recv[:, cols].astype(F32)
        g_ref[0, x, :, :, :, :, cols] = own.astype(BF16).reshape(TILES, NY, NK, SHARE, HD)
    q_first = gather(0)
    dv_near.wait_recv()
    dv_far.wait_recv()
    join(1)
    v_first = gather(2)
    x_side.wait_recv()
    lax.fori_loop(0, NX * TILES // 2, turn, 0)
    q_last = gather_on(0, q_first)
    dk_near.wait_recv()
    dk_far.wait_recv()
    join(0)
    k_first = gather(1)
    v_last = gather_on(2, v_first)

    w_copy.wait()

    def input_share(core):
        def step(i, carry):
            cols = pl.ds(pl.multiple_of(i * 512, 512), 512)
            part = sum(
                dot(
                    g_ref[a, x, :, :, core].reshape(TILES * NY * SHARE, WIDTH),
                    wv[a, cols, :],
                    NTR,
                )
                for a in range(3)
            )
            gip[core, :, :, :, cols] = part.astype(BF16).reshape(TILES, NY, SHARE, 512)
            return carry

        lax.fori_loop(0, D // 512, step, 0)

    input_share(1 - k)
    cross = push(gip.at[1 - k], gis, sibling)
    for copy in q_last:
        copy.wait_recv()
    shares = weight_share(0)
    k_last = gather_on(1, k_first)
    input_share(k)
    for copy in v_last:
        copy.wait_recv()
    shares += weight_share(2)

    cross.wait_recv()

    def add_cores(i, carry):
        gia[i] = (gip[k, i].astype(F32) + gis[i].astype(F32)).astype(BF16)
        return carry

    lax.fori_loop(0, TILES, add_cores, 0)
    spread = [push(gia.at[:, (y + r) % NY], gir.at[r - 1], y_peer(r)) for r in range(1, NY)]
    for copy in k_last:
        copy.wait_recv()
    shares += weight_share(1)

    for copy in shares:
        copy.wait_recv()
    for a in range(3):
        total = gwp[a, z].astype(F32)
        for r in range(1, NZ):
            total = total + gwr[a, (z + r) % NZ].astype(F32)
        gw_ref[a] = total

    for copy in spread:
        copy.wait_recv()

    def add_chips(i, carry):
        total = gia[i, y].astype(F32)
        for r in range(NY - 1):
            total = total + gir[r, i].astype(F32)
        gi_ref[i] = total.astype(BF16)
        return carry

    lax.fori_loop(0, TILES, add_chips, 0)

    for copy in started:
        copy.wait_send()


N_COPIES = 6 + 3 + 3 + 1 + 1 + 4 + 1 + 3 * 4 + 3 * (NZ - 1) + 1 + 3


def body(normed_input, w_qkv, queries, saved_keys, values, attn_out, grad_out, window_tiles):
    vmem = pl.BlockSpec(memory_space=pltpu.VMEM)
    anywhere = pl.BlockSpec(memory_space=pl.ANY)
    block = (ROWS, WIDTH)
    grads = (3, NX, TILES, NY, NK, SHARE, WIDTH)
    scratch = [
        ((QUERIES, WIDTH), BF16),
        ((QUERIES, WIDTH), BF16),
        ((SLOTS, *block), BF16),
        ((SLOTS, *block), BF16),
        ((HEADS, KEYS, QUERIES), F32),
        ((16, QUERIES), F32),
        ((HEADS * SLOTS, 1, QUERIES), F32),
        ((HEADS * SLOTS, 1, QUERIES), F32),
        ((HEADS * SLOTS, 1, QUERIES), F32),
        ((HEADS, 1, QUERIES), F32),
        ((6, 1, QUERIES), F32),
        ((6, 1, QUERIES), F32),
        ((4, *block), BF16),
        ((4, *block), BF16),
        ((2, *block), F32),
        ((HEADS, HD, QUERIES), F32),
        (block, BF16),
        (block, BF16),
        (grads, BF16),
        ((TILES, NY, SHARE, D), BF16),
        ((NX, TILES, NY, NK, SHARE, DX), BF16),
        ((DX, NX * ROWS), BF16),
        ((3, D, WIDTH), BF16),
        ((3, NZ, DZ, WIDTH), BF16),
        ((3, NZ, DZ, WIDTH), BF16),
        ((NK, TILES, NY, SHARE, D), BF16),
        ((TILES, NY, SHARE, D), BF16),
        ((TILES, NY, SHARE, D), BF16),
        ((NY - 1, TILES, SHARE, D), BF16),
    ]
    grad_input, grad_w = pl.pallas_call(
        kernel,
        out_shape=[
            jax.ShapeDtypeStruct((TILES, SHARE, D), BF16),
            jax.ShapeDtypeStruct((3, DZ, WIDTH), F32),
        ],
        in_specs=[vmem] * 5 + [anywhere] * 2 + [vmem],
        out_specs=[vmem, vmem],
        scratch_shapes=[pltpu.VMEM(shape, kind) for shape, kind in scratch]
        + [
            pltpu.SemaphoreType.DMA((N_COPIES,)),
            pltpu.SemaphoreType.DMA((N_COPIES,)),
            pltpu.SemaphoreType.DMA((3,)),
        ],
        compiler_params=pltpu.CompilerParams(
            collective_id=0, has_side_effects=True, vmem_limit_bytes=60 * 2**20
        ),
        name="window_grads",
    )(
        queries,
        saved_keys,
        values,
        attn_out,
        grad_out,
        normed_input,
        w_qkv.transpose(1, 0, 2),
        window_tiles.T,
    )
    return grad_input, grad_w.transpose(1, 0, 2)


def solution(mesh):
    placed = (
        P("context", "tensor", None),
        P(None, None, "tensor"),
        P("context", "tensor"),
        P("context", "tensor"),
        P("context", "tensor"),
        P("context", "tensor"),
        P("context", "tensor"),
        P(),
    )
    return jax.shard_map(
        body,
        mesh=mesh,
        in_specs=placed,
        out_specs=(P("context", "tensor", None), P("context", None, "tensor")),
        check_vma=False,
    )
```

```python
import functools
import math

import jax
import jax.numpy as jnp
from jax import lax
from jax.experimental import pallas as pl
from jax.experimental.pallas import tpu as pltpu
from jax.sharding import PartitionSpec as P

D = 3072
HD = 128
TILE = 128
NX, NZ, NY, NK = 4, 8, 4, 2
NT, NC = NY * NK, NX * NZ
HEADS = 2
WIDTH = HEADS * HD
TILES = 4
ROWS = TILES * TILE
QUERIES = 2 * ROWS
SLOTS = 3
KEYS = SLOTS * ROWS
SHARE = TILE // NT
DX = D // NX
DZ = DX // NZ
CHUNK = 256
SCALE = 1.0 / math.sqrt(HD)
LOG2E = 1.4426950408889634
MASKED = -1e30
MESH = pl.DeviceIdType.MESH
NN = (((1,), (0,)), ((), ()))
NTR = (((1,), (1,)), ((), ()))
F32 = jnp.float32
BF16 = jnp.bfloat16


def dot(a, b, dims):
    return lax.dot_general(a, b, dims, preferred_element_type=F32)


def kernel(
    q_ref, k_ref, v_ref, o_ref, do_ref, x_ref, w_ref, wt_ref,
    gi_ref, gw_ref,
    qb, dob, kb, vb, e_ref, bias, mx, lx, rx, delta, st_send, st_recv,
    dkv_send, dkv_recv, dkv_own, dqt, dq_send, dq_recv, g_ref,
    xa, xg, xt, wv, gwp, gwr, gip, gis, gia, gib, gir,
    send, recv, local,
):
    t, c = lax.axis_index("tensor"), lax.axis_index("context")
    x, z = c // NZ, c % NZ
    y, k = t // NK, t % NK
    side = 2 * (c % 2) - 1
    partner = c - side
    near = (c + side + NC) % NC
    far = (c + 2 * side + NC) % NC
    far_user = (c - 2 * side + NC) % NC

    def x_peer(r):
        return (t, ((x + r) % NX) * NZ + z)

    def z_peer(r):
        return (t, x * NZ + (z + r) % NZ)

    def y_peer(r):
        return (((y + r) % NY) * NK + k, c)

    sibling = (y * NK + 1 - k, c)

    barrier = pltpu.get_barrier_semaphore()
    peers = [(t, near), (t, far), (t, far_user), sibling]
    peers += [x_peer(r) for r in range(1, NX)]
    peers += [z_peer(r) for r in range(1, NZ)]
    peers += [y_peer(r) for r in range(1, NY)]
    for peer in peers:
        pl.semaphore_signal(barrier, inc=1, device_id=peer, device_id_type=MESH)
    pl.semaphore_wait(barrier, len(peers))

    started = []

    def push(src, dst, device):
        number = len(started)
        copy = pltpu.make_async_remote_copy(
            src_ref=src,
            dst_ref=dst,
            send_sem=send.at[number],
            recv_sem=recv.at[number],
            device_id=device,
            device_id_type=MESH,
        )
        copy.start()
        started.append(copy)
        return copy

    x_first = [
        push(x_ref.at[:, :, pl.ds(((x + r) % NX) * DX, DX)], xa.at[x], x_peer(r))
        for r in range(1, NX)
    ]
    q_swap = push(q_ref, qb.at[pl.ds(ROWS, ROWS)], (t, partner))
    do_swap = push(do_ref, dob.at[pl.ds(ROWS, ROWS)], (t, partner))
    x_own = pltpu.make_async_copy(x_ref.at[:, :, pl.ds(x * DX, DX)], xa.at[x], local.at[0])
    x_own.start()
    w_copy = pltpu.make_async_copy(w_ref, wv, local.at[1])
    w_copy.start()

    qb[pl.ds(0, ROWS), :] = q_ref[...]
    dob[pl.ds(0, ROWS), :] = do_ref[...]
    kb[0] = k_ref[...]
    vb[0] = v_ref[...]

    window = wt_ref[...]
    first_tiles = [c * TILES, near * TILES, far * TILES]
    hits = [
        jnp.max(jnp.where(window == first + i, 1.0, 0.0), axis=0, keepdims=True)
        for first in first_tiles
        for i in range(TILES)
    ]
    hits = jnp.concatenate(hits + [jnp.zeros((4, NC * TILES), F32)], axis=0)
    column = lax.broadcasted_iota(jnp.int32, (NC * TILES, QUERIES), 1) // TILE
    entry = lax.broadcasted_iota(jnp.int32, (NC * TILES, QUERIES), 0)
    wanted = jnp.where(column < TILES, c * TILES + column, partner * TILES + column - TILES)
    pick = jnp.where(entry == wanted, 1.0, 0.0)
    bias[...] = (1.0 - dot(hits.astype(BF16), pick.astype(BF16), NN)) * MASKED

    st_send[...] = jnp.zeros_like(st_send)
    for h in range(HEADS):
        cols = pl.ds(h * HD, HD)
        product = do_ref[:, cols].astype(F32) * o_ref[:, cols].astype(F32)
        row = jnp.sum(product.T, axis=0, keepdims=True)
        delta[h, :, pl.ds(0, ROWS)] = row
        st_send[4 + h, :, pl.ds(0, ROWS)] = row

    def score_block(slot, first, count):
        def step(i, carry):
            h = i // count
            cols = pl.ds(pl.multiple_of((first + i % count) * CHUNK, CHUNK), CHUNK)
            head = pl.ds(pl.multiple_of(h * HD, HD), HD)
            s = dot(kb[slot, :, head], qb[cols, head], NTR) * (SCALE * LOG2E)
            parts = [
                s[i * TILE : (i + 1) * TILE] + bias[pl.ds(slot * TILES + i, 1), cols]
                for i in range(TILES)
            ]
            top = functools.reduce(jnp.maximum, parts)
            top = jnp.max(top, axis=0, keepdims=True)
            total = None
            for i, part in enumerate(parts):
                e = jnp.exp2(part - top)
                e_ref[h, pl.ds(slot * ROWS + i * TILE, TILE), cols] = e
                total = e if total is None else total + e
            mx[h * SLOTS + slot, :, cols] = top
            lx[h * SLOTS + slot, :, cols] = jnp.sum(total, axis=0, keepdims=True)
            return carry

        lax.fori_loop(0, HEADS * count, step, 0)

    x_own.wait()
    for copy in x_first:
        copy.wait_recv()
    k_near = push(k_ref, kb.at[1], (t, near))
    k_far = push(k_ref, kb.at[2], (t, far_user))
    v_near = push(v_ref, vb.at[1], (t, near))
    x_second = [push(xa, xg.at[:, :, y, k], y_peer(r)) for r in range(1, NY)]
    x_place = pltpu.make_async_copy(xa, xg.at[:, :, y, k], local.at[2])
    x_place.start()

    half = ROWS // CHUNK
    score_block(0, 0, half)

    q_swap.wait_recv()
    score_block(0, half, half)
    k_near.wait_recv()
    score_block(1, 0, 2 * half)
    k_far.wait_recv()
    score_block(2, 0, 2 * half)

    for h in range(HEADS):
        tops = [mx[h * SLOTS + j] for j in range(SLOTS)]
        top = functools.reduce(jnp.maximum, tops)
        total = sum(lx[h * SLOTS + j] * jnp.exp2(tops[j] - top) for j in range(SLOTS))
        st_send[h] = top
        st_send[2 + h] = total
    stats = push(st_send, st_recv, (t, partner))
    v_far = push(v_ref, vb.at[2], (t, far_user))
    dqt[...] = jnp.zeros_like(dqt)

    stats.wait_recv()
    for h in range(HEADS):
        delta[h, :, pl.ds(ROWS, ROWS)] = st_recv[4 + h, :, pl.ds(0, ROWS)]
        for u in range(2):
            mine, theirs = pl.ds(u * ROWS, ROWS), pl.ds((1 - u) * ROWS, ROWS)
            top_a, top_b = st_send[h, :, mine], st_recv[h, :, theirs]
            top = jnp.maximum(top_a, top_b)
            total = st_send[2 + h, :, mine] * jnp.exp2(top_a - top)
            total = total + st_recv[2 + h, :, theirs] * jnp.exp2(top_b - top)
            lse = top + jnp.log2(total)
            for j in range(SLOTS):
                rx[h * SLOTS + j, :, mine] = jnp.exp2(mx[h * SLOTS + j, :, mine] - lse)

    def grad_block(slot):
        def step(i, carry):
            h = i // 2
            part = pl.multiple_of((i % 2) * CHUNK, CHUNK)
            head = pl.ds(pl.multiple_of(h * HD, HD), HD)
            here = pl.ds(part, CHUNK)
            rows = pl.ds(slot * ROWS + part, CHUNK)
            keys_t = kb[slot, here, head].T
            value = vb[slot, here, head]
            grad_k = grad_v = None
            for u in range(2):
                cols = pl.ds(u * ROWS, ROWS)
                p = e_ref[h, rows, cols] * rx[h * SLOTS + slot, :, cols]
                dp = dot(value, dob[cols, head], NTR)
                ds = (p * (dp - delta[h, :, cols])).astype(BF16)
                dv = dot(p.astype(BF16), dob[cols, head], NN)
                dk = dot(ds, qb[cols, head], NN)
                grad_v = dv if grad_v is None else grad_v + dv
                grad_k = dk if grad_k is None else grad_k + dk
                dqt[h, :, cols] += dot(keys_t, ds, NN)
            if slot == 0:
                dkv_own[0, here, head] = grad_k * SCALE
                dkv_own[1, here, head] = grad_v
            else:
                dkv_send[2 * slot - 2, here, head] = (grad_k * SCALE).astype(BF16)
                dkv_send[2 * slot - 1, here, head] = grad_v.astype(BF16)
            return carry

        lax.fori_loop(0, HEADS * 2, step, 0)

    do_swap.wait_recv()
    v_near.wait_recv()
    grad_block(1)
    dv_near = push(dkv_send.at[1], dkv_recv.at[1], (t, near))
    dk_near = push(dkv_send.at[0], dkv_recv.at[0], (t, near))

    v_far.wait_recv()
    grad_block(2)
    dv_far = push(dkv_send.at[3], dkv_recv.at[3], (t, far))
    dk_far = push(dkv_send.at[2], dkv_recv.at[2], (t, far))
    grad_block(0)
    for h in range(HEADS):
        dq_send[:, pl.ds(h * HD, HD)] = (dqt[h, :, pl.ds(ROWS, ROWS)] * SCALE).T.astype(BF16)
    dq_swap = push(dq_send, dq_recv, (t, partner))

    def turn(i, carry):
        for u in range(2):
            block = xg[i // 2, (i % 2) * 2 + u].reshape(TILE, DX)
            xt[:, pl.ds(pl.multiple_of(i * 2 * TILE, 2 * TILE) + u * TILE, TILE)] = block.T
        return carry

    def gather(a):
        return [push(g_ref.at[a, x], g_ref.at[a, x], x_peer(r)) for r in (1, NX - 1)]

    def gather_on(a, first):
        copies = []
        for copy, r, part in zip(first, (1, NX - 1), (0, TILES // 2)):
            copy.wait_recv()
            piece = g_ref.at[a, (x - r + NX) % NX, pl.ds(part, TILES // 2)]
            copies.append(push(piece, piece, x_peer(r)))
        return copies

    def weight_share(a):
        def step(i, carry):
            rows = pl.ds(pl.multiple_of(i * 2 * DZ, 2 * DZ), 2 * DZ)
            part = dot(xt[rows, :], g_ref[a].reshape(NX * ROWS, WIDTH), NN)
            gwp[a, pl.ds(2 * i, 2)] = part.reshape(2, DZ, WIDTH).astype(BF16)
            return carry

        lax.fori_loop(0, NZ // 2, step, 0)
        return [push(gwp.at[a, (z + r) % NZ], gwr.at[a, z], z_peer(r)) for r in range(1, NZ)]

    def join(a):
        total = dkv_own[a] + dkv_recv[a].astype(F32) + dkv_recv[2 + a].astype(F32)
        g_ref[1 + a, x] = total.astype(BF16).reshape(TILES, NY, NK, SHARE, WIDTH)

    dq_swap.wait_recv()
    for h in range(HEADS):
        cols = pl.ds(h * HD, HD)
        own = (dqt[h, :, pl.ds(0, ROWS)] * SCALE).T + dq_recv[:, cols].astype(F32)
        g_ref[0, x, :, :, :, :, cols] = own.astype(BF16).reshape(TILES, NY, NK, SHARE, HD)
    q_first = gather(0)

    x_place.wait()
    for copy in x_second:
        copy.wait_recv()
    x_side = push(xg.at[:, :, :, k], xg.at[:, :, :, k], sibling)

    dv_near.wait_recv()
    dv_far.wait_recv()
    join(1)
    v_first = gather(2)
    x_side.wait_recv()
    lax.fori_loop(0, NX * TILES // 2, turn, 0)
    q_last = gather_on(0, q_first)
    dk_near.wait_recv()
    dk_far.wait_recv()
    join(0)
    k_first = gather(1)

    w_copy.wait()
    part_cols = [pl.ds(i * (D // 2), D // 2) for i in range(2)]

    def input_share(core, part):
        def step(i, carry):
            cols = pl.ds(pl.multiple_of(part * (D // 2) + i * 512, 512), 512)
            total = sum(
                dot(
                    g_ref[a, x, :, :, core].reshape(TILES * NY * SHARE, WIDTH),
                    wv[a, cols, :],
                    NTR,
                )
                for a in range(3)
            )
            gip[core, :, :, :, cols] = total.astype(BF16).reshape(TILES, NY, SHARE, 512)
            return carry

        lax.fori_loop(0, D // 1024, step, 0)

    cross = []
    for i, cols in enumerate(part_cols):
        input_share(1 - k, i)
        cross.append(push(gip.at[1 - k, :, :, :, cols], gis.at[:, :, :, cols], sibling))
    for copy in q_last:
        copy.wait_recv()
    shares = weight_share(0)
    v_last = gather_on(2, v_first)
    for i in range(2):
        input_share(k, i)

    up, down = (y + 1) % NY, (y + NY - 1) % NY
    ahead, early, late = [], [], []
    for i, cols in enumerate(part_cols):
        cross[i].wait_recv()

        def add_cores(j, carry):
            both = gip[k, j, :, :, cols].astype(F32) + gis[j, :, :, cols].astype(F32)
            gia[j, :, :, cols] = both.astype(BF16)
            return carry

        lax.fori_loop(0, TILES, add_cores, 0)
        forth, back = (y_peer(1), y_peer(NY - 1)) if i == 0 else (y_peer(NY - 1), y_peer(1))
        near_by = down if i == 0 else up
        ahead.append(push(gia.at[:, (y + 2) % NY, :, cols], gib.at[i], forth))
        early.append(push(gia.at[:, near_by, :, cols], gir.at[1 - i, :, :, cols], back))

    k_last = gather_on(1, k_first)
    for copy in v_last:
        copy.wait_recv()
    shares += weight_share(2)
    for i, cols in enumerate(part_cols):
        ahead[i].wait_recv()
        near_by = up if i == 0 else down
        through = gia[:, near_by, :, cols].astype(F32) + gib[i].astype(F32)
        gia[:, near_by, :, cols] = through.astype(BF16)
        forth = y_peer(1) if i == 0 else y_peer(NY - 1)
        late.append(push(gia.at[:, near_by, :, cols], gir.at[i, :, :, cols], forth))
    for copy in k_last:
        copy.wait_recv()
    shares += weight_share(1)

    for copy in shares:
        copy.wait_recv()
    for a in range(3):
        total = gwp[a, z].astype(F32)
        for r in range(1, NZ):
            total = total + gwr[a, (z + r) % NZ].astype(F32)
        gw_ref[a] = total

    for copy in early + late:
        copy.wait_recv()

    def add_chips(i, carry):
        total = gia[i, y].astype(F32)
        for r in range(2):
            total = total + gir[r, i].astype(F32)
        gi_ref[i] = total.astype(BF16)
        return carry

    lax.fori_loop(0, TILES, add_chips, 0)

    for copy in started:
        copy.wait_send()


N_COPIES = 6 + 3 + 3 + 1 + 1 + 4 + 1 + 3 * 4 + 3 * (NZ - 1) + 2 + 6


def body(normed_input, w_qkv, queries, saved_keys, values, attn_out, grad_out, window_tiles):
    vmem = pl.BlockSpec(memory_space=pltpu.VMEM)
    anywhere = pl.BlockSpec(memory_space=pl.ANY)
    block = (ROWS, WIDTH)
    grads = (3, NX, TILES, NY, NK, SHARE, WIDTH)
    scratch = [
        ((QUERIES, WIDTH), BF16),
        ((QUERIES, WIDTH), BF16),
        ((SLOTS, *block), BF16),
        ((SLOTS, *block), BF16),
        ((HEADS, KEYS, QUERIES), F32),
        ((16, QUERIES), F32),
        ((HEADS * SLOTS, 1, QUERIES), F32),
        ((HEADS * SLOTS, 1, QUERIES), F32),
        ((HEADS * SLOTS, 1, QUERIES), F32),
        ((HEADS, 1, QUERIES), F32),
        ((6, 1, QUERIES), F32),
        ((6, 1, QUERIES), F32),
        ((4, *block), BF16),
        ((4, *block), BF16),
        ((2, *block), F32),
        ((HEADS, HD, QUERIES), F32),
        (block, BF16),
        (block, BF16),
        (grads, BF16),
        ((NX, TILES, SHARE, DX), BF16),
        ((NX, TILES, NY, NK, SHARE, DX), BF16),
        ((DX, NX * ROWS), BF16),
        ((3, D, WIDTH), BF16),
        ((3, NZ, DZ, WIDTH), BF16),
        ((3, NZ, DZ, WIDTH), BF16),
        ((NK, TILES, NY, SHARE, D), BF16),
        ((TILES, NY, SHARE, D), BF16),
        ((TILES, NY, SHARE, D), BF16),
        ((2, TILES, SHARE, D // 2), BF16),
        ((2, TILES, SHARE, D), BF16),
    ]
    grad_input, grad_w = pl.pallas_call(
        kernel,
        out_shape=[
            jax.ShapeDtypeStruct((TILES, SHARE, D), BF16),
            jax.ShapeDtypeStruct((3, DZ, WIDTH), F32),
        ],
        in_specs=[vmem] * 6 + [anywhere, vmem],
        out_specs=[vmem, vmem],
        scratch_shapes=[pltpu.VMEM(shape, kind) for shape, kind in scratch]
        + [
            pltpu.SemaphoreType.DMA((N_COPIES,)),
            pltpu.SemaphoreType.DMA((N_COPIES,)),
            pltpu.SemaphoreType.DMA((3,)),
        ],
        compiler_params=pltpu.CompilerParams(
            collective_id=0, has_side_effects=True, vmem_limit_bytes=60 * 2**20
        ),
        name="window_grads",
    )(
        queries,
        saved_keys,
        values,
        attn_out,
        grad_out,
        normed_input,
        w_qkv.transpose(1, 0, 2),
        window_tiles.T,
    )
    return grad_input, grad_w.transpose(1, 0, 2)


def solution(mesh):
    placed = (
        P("context", "tensor", None),
        P(None, None, "tensor"),
        P("context", "tensor"),
        P("context", "tensor"),
        P("context", "tensor"),
        P("context", "tensor"),
        P("context", "tensor"),
        P(),
    )
    return jax.shard_map(
        body,
        mesh=mesh,
        in_specs=placed,
        out_specs=(P("context", "tensor", None), P("context", None, "tensor")),
        check_vma=False,
    )
```

```python
import functools
import math

import jax
import jax.numpy as jnp
from jax import lax
from jax.experimental import pallas as pl
from jax.experimental.pallas import tpu as pltpu
from jax.sharding import PartitionSpec as P

D = 3072
HD = 128
TILE = 128
NX, NZ, NY, NK = 4, 8, 4, 2
NT, NC = NY * NK, NX * NZ
HEADS = 2
WIDTH = HEADS * HD
TILES = 4
ROWS = TILES * TILE
QUERIES = 2 * ROWS
SLOTS = 3
KEYS = SLOTS * ROWS
SHARE = TILE // NT
DX = D // NX
DZ = DX // NZ
CHUNK = 256
SCALE = 1.0 / math.sqrt(HD)
LOG2E = 1.4426950408889634
MASKED = -1e30
MESH = pl.DeviceIdType.MESH
NN = (((1,), (0,)), ((), ()))
NTR = (((1,), (1,)), ((), ()))
F32 = jnp.float32
BF16 = jnp.bfloat16


def dot(a, b, dims):
    return lax.dot_general(a, b, dims, preferred_element_type=F32)


def kernel(
    q_ref, k_ref, v_ref, o_ref, do_ref, x_ref, w_ref, wt_ref,
    gi_ref, gw_ref,
    qb, dob, kb, vb, e_ref, bias, mx, lx, rx, delta, st_send, st_recv,
    dkv_send, dkv_recv, dkv_own, dqt, dq_send, dq_recv, g_ref,
    xa, xg, xt, wv, gwp, gwr, gip, gis, gia, gib, gir,
    send, recv, local,
):
    t, c = lax.axis_index("tensor"), lax.axis_index("context")
    x, z = c // NZ, c % NZ
    y, k = t // NK, t % NK
    side = 2 * (c % 2) - 1
    partner = c - side
    near = (c + side + NC) % NC
    far = (c + 2 * side + NC) % NC
    far_user = (c - 2 * side + NC) % NC

    def x_peer(r):
        return (t, ((x + r) % NX) * NZ + z)

    def z_peer(r):
        return (t, x * NZ + (z + r) % NZ)

    def y_peer(r):
        return (((y + r) % NY) * NK + k, c)

    sibling = (y * NK + 1 - k, c)

    barrier = pltpu.get_barrier_semaphore()
    peers = [(t, near), (t, far), (t, far_user), sibling]
    peers += [x_peer(r) for r in range(1, NX)]
    peers += [z_peer(r) for r in range(1, NZ)]
    peers += [y_peer(r) for r in range(1, NY)]
    for peer in peers:
        pl.semaphore_signal(barrier, inc=1, device_id=peer, device_id_type=MESH)
    pl.semaphore_wait(barrier, len(peers))

    started = []

    def push(src, dst, device):
        number = len(started)
        copy = pltpu.make_async_remote_copy(
            src_ref=src,
            dst_ref=dst,
            send_sem=send.at[number],
            recv_sem=recv.at[number],
            device_id=device,
            device_id_type=MESH,
        )
        copy.start()
        started.append(copy)
        return copy

    x_first = [
        push(x_ref.at[:, :, pl.ds(((x + r) % NX) * DX, DX)], xa.at[x], x_peer(r))
        for r in range(1, NX)
    ]
    q_swap = push(q_ref, qb.at[pl.ds(ROWS, ROWS)], (t, partner))
    do_swap = push(do_ref, dob.at[pl.ds(ROWS, ROWS)], (t, partner))
    x_own = pltpu.make_async_copy(x_ref.at[:, :, pl.ds(x * DX, DX)], xa.at[x], local.at[0])
    x_own.start()
    w_copy = pltpu.make_async_copy(w_ref, wv, local.at[1])
    w_copy.start()

    qb[pl.ds(0, ROWS), :] = q_ref[...]
    dob[pl.ds(0, ROWS), :] = do_ref[...]
    kb[0] = k_ref[...]
    vb[0] = v_ref[...]

    window = wt_ref[...]
    first_tiles = [c * TILES, near * TILES, far * TILES]
    hits = [
        jnp.max(jnp.where(window == first + i, 1.0, 0.0), axis=0, keepdims=True)
        for first in first_tiles
        for i in range(TILES)
    ]
    hits = jnp.concatenate(hits + [jnp.zeros((4, NC * TILES), F32)], axis=0)
    column = lax.broadcasted_iota(jnp.int32, (NC * TILES, QUERIES), 1) // TILE
    entry = lax.broadcasted_iota(jnp.int32, (NC * TILES, QUERIES), 0)
    wanted = jnp.where(column < TILES, c * TILES + column, partner * TILES + column - TILES)
    pick = jnp.where(entry == wanted, 1.0, 0.0)
    bias[...] = (1.0 - dot(hits.astype(BF16), pick.astype(BF16), NN)) * MASKED

    st_send[...] = jnp.zeros_like(st_send)
    for h in range(HEADS):
        cols = pl.ds(h * HD, HD)
        product = do_ref[:, cols].astype(F32) * o_ref[:, cols].astype(F32)
        row = jnp.sum(product.T, axis=0, keepdims=True)
        delta[h, :, pl.ds(0, ROWS)] = row
        st_send[4 + h, :, pl.ds(0, ROWS)] = row

    def score_block(slot, first, count):
        def step(i, carry):
            h = i // count
            cols = pl.ds(pl.multiple_of((first + i % count) * CHUNK, CHUNK), CHUNK)
            head = pl.ds(pl.multiple_of(h * HD, HD), HD)
            s = dot(kb[slot, :, head], qb[cols, head], NTR) * (SCALE * LOG2E)
            parts = [
                s[i * TILE : (i + 1) * TILE] + bias[pl.ds(slot * TILES + i, 1), cols]
                for i in range(TILES)
            ]
            top = functools.reduce(jnp.maximum, parts)
            top = jnp.max(top, axis=0, keepdims=True)
            total = None
            for i, part in enumerate(parts):
                e = jnp.exp2(part - top)
                e_ref[h, pl.ds(slot * ROWS + i * TILE, TILE), cols] = e
                total = e if total is None else total + e
            mx[h * SLOTS + slot, :, cols] = top
            lx[h * SLOTS + slot, :, cols] = jnp.sum(total, axis=0, keepdims=True)
            return carry

        lax.fori_loop(0, HEADS * count, step, 0)

    x_own.wait()
    for copy in x_first:
        copy.wait_recv()
    k_near = push(k_ref, kb.at[1], (t, near))
    k_far = push(k_ref, kb.at[2], (t, far_user))
    v_near = push(v_ref, vb.at[1], (t, near))
    x_second = [push(xa, xg.at[:, :, y, k], y_peer(r)) for r in range(1, NY)]
    x_place = pltpu.make_async_copy(xa, xg.at[:, :, y, k], local.at[2])
    x_place.start()

    half = ROWS // CHUNK
    score_block(0, 0, half)

    q_swap.wait_recv()
    score_block(0, half, half)
    k_near.wait_recv()
    score_block(1, 0, 2 * half)
    k_far.wait_recv()
    score_block(2, 0, 2 * half)

    for h in range(HEADS):
        tops = [mx[h * SLOTS + j] for j in range(SLOTS)]
        top = functools.reduce(jnp.maximum, tops)
        total = sum(lx[h * SLOTS + j] * jnp.exp2(tops[j] - top) for j in range(SLOTS))
        st_send[h] = top
        st_send[2 + h] = total
    stats = push(st_send, st_recv, (t, partner))
    v_far = push(v_ref, vb.at[2], (t, far_user))
    dqt[...] = jnp.zeros_like(dqt)

    stats.wait_recv()
    for h in range(HEADS):
        delta[h, :, pl.ds(ROWS, ROWS)] = st_recv[4 + h, :, pl.ds(0, ROWS)]
        for u in range(2):
            mine, theirs = pl.ds(u * ROWS, ROWS), pl.ds((1 - u) * ROWS, ROWS)
            top_a, top_b = st_send[h, :, mine], st_recv[h, :, theirs]
            top = jnp.maximum(top_a, top_b)
            total = st_send[2 + h, :, mine] * jnp.exp2(top_a - top)
            total = total + st_recv[2 + h, :, theirs] * jnp.exp2(top_b - top)
            lse = top + jnp.log2(total)
            for j in range(SLOTS):
                rx[h * SLOTS + j, :, mine] = jnp.exp2(mx[h * SLOTS + j, :, mine] - lse)

    def grad_block(slot):
        def step(i, carry):
            h = i // 2
            part = pl.multiple_of((i % 2) * CHUNK, CHUNK)
            head = pl.ds(pl.multiple_of(h * HD, HD), HD)
            here = pl.ds(part, CHUNK)
            rows = pl.ds(slot * ROWS + part, CHUNK)
            keys_t = kb[slot, here, head].T
            value = vb[slot, here, head]
            grad_k = grad_v = None
            for u in range(2):
                cols = pl.ds(u * ROWS, ROWS)
                p = e_ref[h, rows, cols] * rx[h * SLOTS + slot, :, cols]
                dp = dot(value, dob[cols, head], NTR)
                ds = (p * (dp - delta[h, :, cols])).astype(BF16)
                dv = dot(p.astype(BF16), dob[cols, head], NN)
                dk = dot(ds, qb[cols, head], NN)
                grad_v = dv if grad_v is None else grad_v + dv
                grad_k = dk if grad_k is None else grad_k + dk
                dqt[h, :, cols] += dot(keys_t, ds, NN)
            if slot == 0:
                dkv_own[0, here, head] = grad_k * SCALE
                dkv_own[1, here, head] = grad_v
            else:
                dkv_send[2 * slot - 2, here, head] = (grad_k * SCALE).astype(BF16)
                dkv_send[2 * slot - 1, here, head] = grad_v.astype(BF16)
            return carry

        lax.fori_loop(0, HEADS * 2, step, 0)

    do_swap.wait_recv()
    v_near.wait_recv()
    grad_block(1)
    dv_near = push(dkv_send.at[1], dkv_recv.at[1], (t, near))
    dk_near = push(dkv_send.at[0], dkv_recv.at[0], (t, near))

    v_far.wait_recv()
    grad_block(2)
    dv_far = push(dkv_send.at[3], dkv_recv.at[3], (t, far))
    grad_block(0)
    for h in range(HEADS):
        dq_send[:, pl.ds(h * HD, HD)] = (dqt[h, :, pl.ds(ROWS, ROWS)] * SCALE).T.astype(BF16)
    dq_swap = push(dq_send, dq_recv, (t, partner))

    def turn(i, carry):
        for u in range(2):
            block = xg[i // 2, (i % 2) * 2 + u].reshape(TILE, DX)
            xt[:, pl.ds(pl.multiple_of(i * 2 * TILE, 2 * TILE) + u * TILE, TILE)] = block.T
        return carry

    def gather(a):
        return [push(g_ref.at[a, x], g_ref.at[a, x], x_peer(r)) for r in (1, NX - 1)]

    def gather_on(a, first):
        copies = []
        for copy, r, part in zip(first, (1, NX - 1), (0, TILES // 2)):
            copy.wait_recv()
            piece = g_ref.at[a, (x - r + NX) % NX, pl.ds(part, TILES // 2)]
            copies.append(push(piece, piece, x_peer(r)))
        return copies

    def weight_share(a):
        def step(i, carry):
            rows = pl.ds(pl.multiple_of(i * 2 * DZ, 2 * DZ), 2 * DZ)
            part = dot(xt[rows, :], g_ref[a].reshape(NX * ROWS, WIDTH), NN)
            gwp[a, pl.ds(2 * i, 2)] = part.reshape(2, DZ, WIDTH).astype(BF16)
            return carry

        lax.fori_loop(0, NZ // 2, step, 0)
        return [push(gwp.at[a, (z + r) % NZ], gwr.at[a, z], z_peer(r)) for r in range(1, NZ)]

    def join(a):
        total = dkv_own[a] + dkv_recv[a].astype(F32) + dkv_recv[2 + a].astype(F32)
        g_ref[1 + a, x] = total.astype(BF16).reshape(TILES, NY, NK, SHARE, WIDTH)

    dq_swap.wait_recv()
    for h in range(HEADS):
        cols = pl.ds(h * HD, HD)
        own = (dqt[h, :, pl.ds(0, ROWS)] * SCALE).T + dq_recv[:, cols].astype(F32)
        g_ref[0, x, :, :, :, :, cols] = own.astype(BF16).reshape(TILES, NY, NK, SHARE, HD)
    q_first = gather(0)

    x_place.wait()
    for copy in x_second:
        copy.wait_recv()
    x_side = push(xg.at[:, :, :, k], xg.at[:, :, :, k], sibling)

    dv_near.wait_recv()
    dv_far.wait_recv()
    join(1)
    v_first = gather(2)
    dk_far = push(dkv_send.at[2], dkv_recv.at[2], (t, far))
    x_side.wait_recv()
    lax.fori_loop(0, NX * TILES // 2, turn, 0)
    q_last = gather_on(0, q_first)
    dk_near.wait_recv()
    dk_far.wait_recv()
    join(0)
    k_first = gather(1)

    w_copy.wait()
    part_cols = [pl.ds(i * (D // 2), D // 2) for i in range(2)]

    def input_share(core, part):
        def step(i, carry):
            cols = pl.ds(pl.multiple_of(part * (D // 2) + i * 512, 512), 512)
            total = sum(
                dot(
                    g_ref[a, x, :, :, core].reshape(TILES * NY * SHARE, WIDTH),
                    wv[a, cols, :],
                    NTR,
                )
                for a in range(3)
            )
            gip[core, :, :, :, cols] = total.astype(BF16).reshape(TILES, NY, SHARE, 512)
            return carry

        lax.fori_loop(0, D // 1024, step, 0)

    cross = []
    for i, cols in enumerate(part_cols):
        input_share(1 - k, i)
        cross.append(push(gip.at[1 - k, :, :, :, cols], gis.at[:, :, :, cols], sibling))
    for copy in q_last:
        copy.wait_recv()
    shares = weight_share(0)
    v_last = gather_on(2, v_first)
    for i in range(2):
        input_share(k, i)

    up, down = (y + 1) % NY, (y + NY - 1) % NY
    ahead, early, late = [], [], []
    for i, cols in enumerate(part_cols):
        cross[i].wait_recv()

        def add_cores(j, carry):
            both = gip[k, j, :, :, cols].astype(F32) + gis[j, :, :, cols].astype(F32)
            gia[j, :, :, cols] = both.astype(BF16)
            return carry

        lax.fori_loop(0, TILES, add_cores, 0)
        forth, back = (y_peer(1), y_peer(NY - 1)) if i == 0 else (y_peer(NY - 1), y_peer(1))
        near_by = down if i == 0 else up
        ahead.append(push(gia.at[:, (y + 2) % NY, :, cols], gib.at[i], forth))
        early.append(push(gia.at[:, near_by, :, cols], gir.at[1 - i, :, :, cols], back))

    k_last = gather_on(1, k_first)
    for copy in v_last:
        copy.wait_recv()
    shares += weight_share(2)
    for i, cols in enumerate(part_cols):
        ahead[i].wait_recv()
        near_by = up if i == 0 else down
        through = gia[:, near_by, :, cols].astype(F32) + gib[i].astype(F32)
        gia[:, near_by, :, cols] = through.astype(BF16)
        forth = y_peer(1) if i == 0 else y_peer(NY - 1)
        late.append(push(gia.at[:, near_by, :, cols], gir.at[i, :, :, cols], forth))
    for copy in k_last:
        copy.wait_recv()
    shares += weight_share(1)

    for copy in shares:
        copy.wait_recv()
    for a in range(3):
        total = gwp[a, z].astype(F32)
        for r in range(1, NZ):
            total = total + gwr[a, (z + r) % NZ].astype(F32)
        gw_ref[a] = total

    for copy in early + late:
        copy.wait_recv()

    def add_chips(i, carry):
        total = gia[i, y].astype(F32)
        for r in range(2):
            total = total + gir[r, i].astype(F32)
        gi_ref[i] = total.astype(BF16)
        return carry

    lax.fori_loop(0, TILES, add_chips, 0)

    for copy in started:
        copy.wait_send()


N_COPIES = 6 + 3 + 3 + 1 + 1 + 4 + 1 + 3 * 4 + 3 * (NZ - 1) + 2 + 6


def body(normed_input, w_qkv, queries, saved_keys, values, attn_out, grad_out, window_tiles):
    vmem = pl.BlockSpec(memory_space=pltpu.VMEM)
    anywhere = pl.BlockSpec(memory_space=pl.ANY)
    block = (ROWS, WIDTH)
    grads = (3, NX, TILES, NY, NK, SHARE, WIDTH)
    scratch = [
        ((QUERIES, WIDTH), BF16),
        ((QUERIES, WIDTH), BF16),
        ((SLOTS, *block), BF16),
        ((SLOTS, *block), BF16),
        ((HEADS, KEYS, QUERIES), F32),
        ((16, QUERIES), F32),
        ((HEADS * SLOTS, 1, QUERIES), F32),
        ((HEADS * SLOTS, 1, QUERIES), F32),
        ((HEADS * SLOTS, 1, QUERIES), F32),
        ((HEADS, 1, QUERIES), F32),
        ((6, 1, QUERIES), F32),
        ((6, 1, QUERIES), F32),
        ((4, *block), BF16),
        ((4, *block), BF16),
        ((2, *block), F32),
        ((HEADS, HD, QUERIES), F32),
        (block, BF16),
        (block, BF16),
        (grads, BF16),
        ((NX, TILES, SHARE, DX), BF16),
        ((NX, TILES, NY, NK, SHARE, DX), BF16),
        ((DX, NX * ROWS), BF16),
        ((3, D, WIDTH), BF16),
        ((3, NZ, DZ, WIDTH), BF16),
        ((3, NZ, DZ, WIDTH), BF16),
        ((NK, TILES, NY, SHARE, D), BF16),
        ((TILES, NY, SHARE, D), BF16),
        ((TILES, NY, SHARE, D), BF16),
        ((2, TILES, SHARE, D // 2), BF16),
        ((2, TILES, SHARE, D), BF16),
    ]
    grad_input, grad_w = pl.pallas_call(
        kernel,
        out_shape=[
            jax.ShapeDtypeStruct((TILES, SHARE, D), BF16),
            jax.ShapeDtypeStruct((3, DZ, WIDTH), F32),
        ],
        in_specs=[vmem] * 6 + [anywhere, vmem],
        out_specs=[vmem, vmem],
        scratch_shapes=[pltpu.VMEM(shape, kind) for shape, kind in scratch]
        + [
            pltpu.SemaphoreType.DMA((N_COPIES,)),
            pltpu.SemaphoreType.DMA((N_COPIES,)),
            pltpu.SemaphoreType.DMA((3,)),
        ],
        compiler_params=pltpu.CompilerParams(
            collective_id=0, has_side_effects=True, vmem_limit_bytes=60 * 2**20
        ),
        name="window_grads",
    )(
        queries,
        saved_keys,
        values,
        attn_out,
        grad_out,
        normed_input,
        w_qkv.transpose(1, 0, 2),
        window_tiles.T,
    )
    return grad_input, grad_w.transpose(1, 0, 2)


def solution(mesh):
    placed = (
        P("context", "tensor", None),
        P(None, None, "tensor"),
        P("context", "tensor"),
        P("context", "tensor"),
        P("context", "tensor"),
        P("context", "tensor"),
        P("context", "tensor"),
        P(),
    )
    return jax.shard_map(
        body,
        mesh=mesh,
        in_specs=placed,
        out_specs=(P("context", "tensor", None), P("context", None, "tensor")),
        check_vma=False,
    )
```

```python
import functools
import math

import jax
import jax.numpy as jnp
from jax import lax
from jax.experimental import pallas as pl
from jax.experimental.pallas import tpu as pltpu
from jax.sharding import PartitionSpec as P

D = 3072
HD = 128
TILE = 128
NX, NZ, NY, NK = 4, 8, 4, 2
NT, NC = NY * NK, NX * NZ
HEADS = 2
WIDTH = HEADS * HD
TILES = 4
ROWS = TILES * TILE
QUERIES = 2 * ROWS
SLOTS = 3
KEYS = SLOTS * ROWS
SHARE = TILE // NT
DX = D // NX
DZ = DX // NZ
CHUNK = 256
SCALE = 1.0 / math.sqrt(HD)
LOG2E = 1.4426950408889634
MASKED = -1e30
MESH = pl.DeviceIdType.MESH
NN = (((1,), (0,)), ((), ()))
NTR = (((1,), (1,)), ((), ()))
F32 = jnp.float32
BF16 = jnp.bfloat16


def dot(a, b, dims):
    return lax.dot_general(a, b, dims, preferred_element_type=F32)


def kernel(
    q_ref, k_ref, v_ref, o_ref, do_ref, x_ref, w_ref, wt_ref,
    gi_ref, gw_ref,
    qb, dob, kb, vb, e_ref, bias, mx, lx, rx, delta, st_send, st_recv,
    dkv_send, dkv_recv, dkv_own, dqt, dq_send, dq_recv, g_ref,
    xa, xg, xt, wv, gwp, gwr, gip, gis, gia, gib, gir,
    send, recv, local,
):
    t, c = lax.axis_index("tensor"), lax.axis_index("context")
    x, z = c // NZ, c % NZ
    y, k = t // NK, t % NK
    side = 2 * (c % 2) - 1
    partner = c - side
    near = (c + side + NC) % NC
    far = (c + 2 * side + NC) % NC
    far_user = (c - 2 * side + NC) % NC

    def x_peer(r):
        return (t, ((x + r) % NX) * NZ + z)

    def z_peer(r):
        return (t, x * NZ + (z + r) % NZ)

    def y_peer(r):
        return (((y + r) % NY) * NK + k, c)

    sibling = (y * NK + 1 - k, c)

    barrier = pltpu.get_barrier_semaphore()
    peers = [(t, near), (t, far), (t, far_user), sibling]
    peers += [x_peer(r) for r in range(1, NX)]
    peers += [z_peer(r) for r in range(1, NZ)]
    peers += [y_peer(r) for r in range(1, NY)]
    for peer in peers:
        pl.semaphore_signal(barrier, inc=1, device_id=peer, device_id_type=MESH)
    pl.semaphore_wait(barrier, len(peers))

    started = []

    def push(src, dst, device):
        number = len(started)
        copy = pltpu.make_async_remote_copy(
            src_ref=src,
            dst_ref=dst,
            send_sem=send.at[number],
            recv_sem=recv.at[number],
            device_id=device,
            device_id_type=MESH,
        )
        copy.start()
        started.append(copy)
        return copy

    x_first = [
        push(x_ref.at[:, :, pl.ds(((x + r) % NX) * DX, DX)], xa.at[x], x_peer(r))
        for r in range(1, NX)
    ]
    q_swap = push(q_ref, qb.at[pl.ds(ROWS, ROWS)], (t, partner))
    do_swap = push(do_ref, dob.at[pl.ds(ROWS, ROWS)], (t, partner))
    x_own = pltpu.make_async_copy(x_ref.at[:, :, pl.ds(x * DX, DX)], xa.at[x], local.at[0])
    x_own.start()
    w_copy = pltpu.make_async_copy(w_ref, wv, local.at[1])
    w_copy.start()

    qb[pl.ds(0, ROWS), :] = q_ref[...]
    dob[pl.ds(0, ROWS), :] = do_ref[...]
    kb[0] = k_ref[...]
    vb[0] = v_ref[...]

    window = wt_ref[...]
    first_tiles = [c * TILES, near * TILES, far * TILES]
    hits = [
        jnp.max(jnp.where(window == first + i, 1.0, 0.0), axis=0, keepdims=True)
        for first in first_tiles
        for i in range(TILES)
    ]
    hits = jnp.concatenate(hits + [jnp.zeros((4, NC * TILES), F32)], axis=0)
    column = lax.broadcasted_iota(jnp.int32, (NC * TILES, QUERIES), 1) // TILE
    entry = lax.broadcasted_iota(jnp.int32, (NC * TILES, QUERIES), 0)
    wanted = jnp.where(column < TILES, c * TILES + column, partner * TILES + column - TILES)
    pick = jnp.where(entry == wanted, 1.0, 0.0)
    bias[...] = (1.0 - dot(hits.astype(BF16), pick.astype(BF16), NN)) * MASKED

    st_send[...] = jnp.zeros_like(st_send)
    for h in range(HEADS):
        cols = pl.ds(h * HD, HD)
        product = do_ref[:, cols].astype(F32) * o_ref[:, cols].astype(F32)
        row = jnp.sum(product.T, axis=0, keepdims=True)
        delta[h, :, pl.ds(0, ROWS)] = row
        st_send[4 + h, :, pl.ds(0, ROWS)] = row

    def score_block(slot, first, count):
        def step(i, carry):
            h = i // count
            cols = pl.ds(pl.multiple_of((first + i % count) * CHUNK, CHUNK), CHUNK)
            head = pl.ds(pl.multiple_of(h * HD, HD), HD)
            s = dot(kb[slot, :, head], qb[cols, head], NTR) * (SCALE * LOG2E)
            parts = [
                s[i * TILE : (i + 1) * TILE] + bias[pl.ds(slot * TILES + i, 1), cols]
                for i in range(TILES)
            ]
            top = functools.reduce(jnp.maximum, parts)
            top = jnp.max(top, axis=0, keepdims=True)
            total = None
            for i, part in enumerate(parts):
                e = jnp.exp2(part - top)
                e_ref[h, pl.ds(slot * ROWS + i * TILE, TILE), cols] = e
                total = e if total is None else total + e
            mx[h * SLOTS + slot, :, cols] = top
            lx[h * SLOTS + slot, :, cols] = jnp.sum(total, axis=0, keepdims=True)
            return carry

        lax.fori_loop(0, HEADS * count, step, 0)

    x_own.wait()
    for copy in x_first:
        copy.wait_recv()
    k_near = push(k_ref, kb.at[1], (t, near))
    k_far = push(k_ref, kb.at[2], (t, far_user))
    v_near = push(v_ref, vb.at[1], (t, near))
    x_second = [push(xa, xg.at[:, :, y, k], y_peer(r)) for r in range(1, NY)]
    x_place = pltpu.make_async_copy(xa, xg.at[:, :, y, k], local.at[2])
    x_place.start()

    half = ROWS // CHUNK
    score_block(0, 0, half)

    q_swap.wait_recv()
    score_block(0, half, half)
    k_near.wait_recv()
    score_block(1, 0, 2 * half)
    k_far.wait_recv()
    score_block(2, 0, 2 * half)

    for h in range(HEADS):
        tops = [mx[h * SLOTS + j] for j in range(SLOTS)]
        top = functools.reduce(jnp.maximum, tops)
        total = sum(lx[h * SLOTS + j] * jnp.exp2(tops[j] - top) for j in range(SLOTS))
        st_send[h] = top
        st_send[2 + h] = total
    stats = push(st_send, st_recv, (t, partner))
    v_far = push(v_ref, vb.at[2], (t, far_user))
    dqt[...] = jnp.zeros_like(dqt)

    stats.wait_recv()
    for h in range(HEADS):
        delta[h, :, pl.ds(ROWS, ROWS)] = st_recv[4 + h, :, pl.ds(0, ROWS)]
        for u in range(2):
            mine, theirs = pl.ds(u * ROWS, ROWS), pl.ds((1 - u) * ROWS, ROWS)
            top_a, top_b = st_send[h, :, mine], st_recv[h, :, theirs]
            top = jnp.maximum(top_a, top_b)
            total = st_send[2 + h, :, mine] * jnp.exp2(top_a - top)
            total = total + st_recv[2 + h, :, theirs] * jnp.exp2(top_b - top)
            lse = top + jnp.log2(total)
            for j in range(SLOTS):
                rx[h * SLOTS + j, :, mine] = jnp.exp2(mx[h * SLOTS + j, :, mine] - lse)

    def grad_block(slot):
        def step(i, carry):
            h = i // 2
            part = pl.multiple_of((i % 2) * CHUNK, CHUNK)
            head = pl.ds(pl.multiple_of(h * HD, HD), HD)
            here = pl.ds(part, CHUNK)
            rows = pl.ds(slot * ROWS + part, CHUNK)
            keys_t = kb[slot, here, head].T
            value = vb[slot, here, head]
            grad_k = grad_v = None
            for u in range(2):
                cols = pl.ds(u * ROWS, ROWS)
                p = e_ref[h, rows, cols] * rx[h * SLOTS + slot, :, cols]
                dp = dot(value, dob[cols, head], NTR)
                ds = (p * (dp - delta[h, :, cols])).astype(BF16)
                dv = dot(p.astype(BF16), dob[cols, head], NN)
                dk = dot(ds, qb[cols, head], NN)
                grad_v = dv if grad_v is None else grad_v + dv
                grad_k = dk if grad_k is None else grad_k + dk
                dqt[h, :, cols] += dot(keys_t, ds, NN)
            if slot == 0:
                dkv_own[0, here, head] = grad_k * SCALE
                dkv_own[1, here, head] = grad_v
            else:
                dkv_send[2 * slot - 2, here, head] = (grad_k * SCALE).astype(BF16)
                dkv_send[2 * slot - 1, here, head] = grad_v.astype(BF16)
            return carry

        lax.fori_loop(0, HEADS * 2, step, 0)

    do_swap.wait_recv()
    v_near.wait_recv()
    grad_block(1)
    dv_near = push(dkv_send.at[1], dkv_recv.at[1], (t, near))

    v_far.wait_recv()
    grad_block(2)
    dv_far = push(dkv_send.at[3], dkv_recv.at[3], (t, far))
    dk_near = push(dkv_send.at[0], dkv_recv.at[0], (t, near))
    grad_block(0)
    for h in range(HEADS):
        dq_send[:, pl.ds(h * HD, HD)] = (dqt[h, :, pl.ds(ROWS, ROWS)] * SCALE).T.astype(BF16)
    dq_swap = push(dq_send, dq_recv, (t, partner))

    def turn(i, carry):
        for u in range(2):
            block = xg[i // 2, (i % 2) * 2 + u].reshape(TILE, DX)
            xt[:, pl.ds(pl.multiple_of(i * 2 * TILE, 2 * TILE) + u * TILE, TILE)] = block.T
        return carry

    def gather(a):
        return [push(g_ref.at[a, x], g_ref.at[a, x], x_peer(r)) for r in (1, NX - 1)]

    def gather_on(a, first):
        copies = []
        for copy, r, part in zip(first, (1, NX - 1), (0, TILES // 2)):
            copy.wait_recv()
            piece = g_ref.at[a, (x - r + NX) % NX, pl.ds(part, TILES // 2)]
            copies.append(push(piece, piece, x_peer(r)))
        return copies

    def weight_share(a):
        def step(i, carry):
            rows = pl.ds(pl.multiple_of(i * 2 * DZ, 2 * DZ), 2 * DZ)
            part = dot(xt[rows, :], g_ref[a].reshape(NX * ROWS, WIDTH), NN)
            gwp[a, pl.ds(2 * i, 2)] = part.reshape(2, DZ, WIDTH).astype(BF16)
            return carry

        lax.fori_loop(0, NZ // 2, step, 0)
        return [push(gwp.at[a, (z + r) % NZ], gwr.at[a, z], z_peer(r)) for r in range(1, NZ)]

    def join(a):
        total = dkv_own[a] + dkv_recv[a].astype(F32) + dkv_recv[2 + a].astype(F32)
        g_ref[1 + a, x] = total.astype(BF16).reshape(TILES, NY, NK, SHARE, WIDTH)

    dq_swap.wait_recv()
    for h in range(HEADS):
        cols = pl.ds(h * HD, HD)
        own = (dqt[h, :, pl.ds(0, ROWS)] * SCALE).T + dq_recv[:, cols].astype(F32)
        g_ref[0, x, :, :, :, :, cols] = own.astype(BF16).reshape(TILES, NY, NK, SHARE, HD)
    q_first = gather(0)

    x_place.wait()
    for copy in x_second:
        copy.wait_recv()
    x_side = push(xg.at[:, :, :, k], xg.at[:, :, :, k], sibling)

    dv_near.wait_recv()
    dv_far.wait_recv()
    join(1)
    v_first = gather(2)
    dk_far = push(dkv_send.at[2], dkv_recv.at[2], (t, far))
    x_side.wait_recv()
    lax.fori_loop(0, NX * TILES // 2, turn, 0)
    q_last = gather_on(0, q_first)
    dk_near.wait_recv()
    dk_far.wait_recv()
    join(0)
    k_first = gather(1)

    w_copy.wait()
    part_cols = [pl.ds(i * (D // 2), D // 2) for i in range(2)]

    def input_share(core, part):
        def step(i, carry):
            cols = pl.ds(pl.multiple_of(part * (D // 2) + i * 512, 512), 512)
            total = sum(
                dot(
                    g_ref[a, x, :, :, core].reshape(TILES * NY * SHARE, WIDTH),
                    wv[a, cols, :],
                    NTR,
                )
                for a in range(3)
            )
            gip[core, :, :, :, cols] = total.astype(BF16).reshape(TILES, NY, SHARE, 512)
            return carry

        lax.fori_loop(0, D // 1024, step, 0)

    cross = []
    for i, cols in enumerate(part_cols):
        input_share(1 - k, i)
        cross.append(push(gip.at[1 - k, :, :, :, cols], gis.at[:, :, :, cols], sibling))
    for copy in q_last:
        copy.wait_recv()
    shares = weight_share(0)
    v_last = gather_on(2, v_first)
    for i in range(2):
        input_share(k, i)

    up, down = (y + 1) % NY, (y + NY - 1) % NY
    ahead, early, late = [], [], []
    for i, cols in enumerate(part_cols):
        cross[i].wait_recv()

        def add_cores(j, carry):
            both = gip[k, j, :, :, cols].astype(F32) + gis[j, :, :, cols].astype(F32)
            gia[j, :, :, cols] = both.astype(BF16)
            return carry

        lax.fori_loop(0, TILES, add_cores, 0)
        forth, back = (y_peer(1), y_peer(NY - 1)) if i == 0 else (y_peer(NY - 1), y_peer(1))
        near_by = down if i == 0 else up
        ahead.append(push(gia.at[:, (y + 2) % NY, :, cols], gib.at[i], forth))
        early.append(push(gia.at[:, near_by, :, cols], gir.at[1 - i, :, :, cols], back))

    k_last = gather_on(1, k_first)
    for copy in v_last:
        copy.wait_recv()
    shares += weight_share(2)
    for i, cols in enumerate(part_cols):
        ahead[i].wait_recv()
        near_by = up if i == 0 else down
        through = gia[:, near_by, :, cols].astype(F32) + gib[i].astype(F32)
        gia[:, near_by, :, cols] = through.astype(BF16)
        forth = y_peer(1) if i == 0 else y_peer(NY - 1)
        late.append(push(gia.at[:, near_by, :, cols], gir.at[i, :, :, cols], forth))
    for copy in k_last:
        copy.wait_recv()
    shares += weight_share(1)

    for copy in shares:
        copy.wait_recv()
    for a in range(3):
        total = gwp[a, z].astype(F32)
        for r in range(1, NZ):
            total = total + gwr[a, (z + r) % NZ].astype(F32)
        gw_ref[a] = total

    for copy in early + late:
        copy.wait_recv()

    def add_chips(i, carry):
        total = gia[i, y].astype(F32)
        for r in range(2):
            total = total + gir[r, i].astype(F32)
        gi_ref[i] = total.astype(BF16)
        return carry

    lax.fori_loop(0, TILES, add_chips, 0)

    for copy in started:
        copy.wait_send()


N_COPIES = 6 + 3 + 3 + 1 + 1 + 4 + 1 + 3 * 4 + 3 * (NZ - 1) + 2 + 6


def body(normed_input, w_qkv, queries, saved_keys, values, attn_out, grad_out, window_tiles):
    vmem = pl.BlockSpec(memory_space=pltpu.VMEM)
    anywhere = pl.BlockSpec(memory_space=pl.ANY)
    block = (ROWS, WIDTH)
    grads = (3, NX, TILES, NY, NK, SHARE, WIDTH)
    scratch = [
        ((QUERIES, WIDTH), BF16),
        ((QUERIES, WIDTH), BF16),
        ((SLOTS, *block), BF16),
        ((SLOTS, *block), BF16),
        ((HEADS, KEYS, QUERIES), F32),
        ((16, QUERIES), F32),
        ((HEADS * SLOTS, 1, QUERIES), F32),
        ((HEADS * SLOTS, 1, QUERIES), F32),
        ((HEADS * SLOTS, 1, QUERIES), F32),
        ((HEADS, 1, QUERIES), F32),
        ((6, 1, QUERIES), F32),
        ((6, 1, QUERIES), F32),
        ((4, *block), BF16),
        ((4, *block), BF16),
        ((2, *block), F32),
        ((HEADS, HD, QUERIES), F32),
        (block, BF16),
        (block, BF16),
        (grads, BF16),
        ((NX, TILES, SHARE, DX), BF16),
        ((NX, TILES, NY, NK, SHARE, DX), BF16),
        ((DX, NX * ROWS), BF16),
        ((3, D, WIDTH), BF16),
        ((3, NZ, DZ, WIDTH), BF16),
        ((3, NZ, DZ, WIDTH), BF16),
        ((NK, TILES, NY, SHARE, D), BF16),
        ((TILES, NY, SHARE, D), BF16),
        ((TILES, NY, SHARE, D), BF16),
        ((2, TILES, SHARE, D // 2), BF16),
        ((2, TILES, SHARE, D), BF16),
    ]
    grad_input, grad_w = pl.pallas_call(
        kernel,
        out_shape=[
            jax.ShapeDtypeStruct((TILES, SHARE, D), BF16),
            jax.ShapeDtypeStruct((3, DZ, WIDTH), F32),
        ],
        in_specs=[vmem] * 6 + [anywhere, vmem],
        out_specs=[vmem, vmem],
        scratch_shapes=[pltpu.VMEM(shape, kind) for shape, kind in scratch]
        + [
            pltpu.SemaphoreType.DMA((N_COPIES,)),
            pltpu.SemaphoreType.DMA((N_COPIES,)),
            pltpu.SemaphoreType.DMA((3,)),
        ],
        compiler_params=pltpu.CompilerParams(
            collective_id=0, has_side_effects=True, vmem_limit_bytes=60 * 2**20
        ),
        name="window_grads",
    )(
        queries,
        saved_keys,
        values,
        attn_out,
        grad_out,
        normed_input,
        w_qkv.transpose(1, 0, 2),
        window_tiles.T,
    )
    return grad_input, grad_w.transpose(1, 0, 2)


def solution(mesh):
    placed = (
        P("context", "tensor", None),
        P(None, None, "tensor"),
        P("context", "tensor"),
        P("context", "tensor"),
        P("context", "tensor"),
        P("context", "tensor"),
        P("context", "tensor"),
        P(),
    )
    return jax.shard_map(
        body,
        mesh=mesh,
        in_specs=placed,
        out_specs=(P("context", "tensor", None), P("context", None, "tensor")),
        check_vma=False,
    )
```
